128 devices in a mesh: mode: 8 (over y, x_hi), col: 16 (over x_lo, z, core).
Axes of the slice: x: 4 (x_hi: 2, x_lo: 2; x = x_hi * 2 + x_lo), y: 4, z: 4, core: 2. Of those that a mesh axis runs over, the one named last changes fastest.
Arguments:
- fields: float32 [2, 288, 64, 4096], P(None, 'mode', None, 'col'), may hold values from -6 to 6
- evaluate: bfloat16 [1584, 288], replicated, may hold values from -0.375 to 0.375
- project: bfloat16 [288, 1584], replicated, may hold values from -0.15625 to 0.15625
- feed: float32 [1584], replicated, may hold values from 0.02 to 0.2
- kill: float32 [1584], replicated, may hold values from 0.04 to 0.4
Outputs:
- stepped: float32 [2, 288, 64, 4096], P(None, 'mode', None, 'col')
The draws below stay inside these ranges and needn't reach their ends.
All inputs are finite; a program needn't handle non-finite values.
Results may differ from the reference program's by a relative error of at most 0.0039.
Values may be sent and summed in bfloat16 or wider, within the bound.
A program may use at most 384 MiB of HBM per device.

```python
import math
import jax
import jax.numpy as jnp
from jax import lax

MODES = 288
POINTS = 1584
ROWS = 64
SWEEPS = 4
COLS = 4096


def steps_of(rng, extent, cuts, least, high):
    def one(dim, blocks):
        steps = jax.random.uniform(jax.random.fold_in(jax.random.fold_in(rng, 6), dim), (blocks,), jnp.float32, least / len(cuts), high / len(cuts))
        return jnp.repeat(jnp.exp(steps), extent[dim] // blocks).reshape((-1,) + (1,) * (len(extent) - dim - 1))

    factor_of = one(*cuts[0])
    for cut in cuts[1:]:
        factor_of = factor_of * one(*cut)
    return factor_of


def bell_draw(own_key, dims, spread, limit, cuts=(), kind=jnp.bfloat16):
    values = jax.random.normal(own_key, dims, jnp.float32) * spread
    if len(cuts) > 0:
        values = steps_of(own_key, dims, cuts, -0.22, 0.18) * values
    return jnp.clip(values, min=-limit, max=limit).astype(kind)


def setup_inputs(seed: int = 0) -> dict:
    key_of = jax.random.split(jax.random.key(seed), 6)
    fields = bell_draw(key_of[0], (2, MODES, ROWS, COLS), 1.0, 6.0, ((1, 8), (3, 16)), jnp.float32)
    evaluate = bell_draw(key_of[1], (POINTS, MODES), MODES ** -0.5, 0.375)
    project = bell_draw(key_of[2], (MODES, POINTS), POINTS ** -0.5, 0.15625)
    feed = jnp.clip(jnp.exp(jax.random.uniform(key_of[3], (POINTS,), jnp.float32, math.log(0.02), math.log(0.2))), 0.02, 0.2)
    kill = jnp.clip(jnp.exp(jax.random.uniform(key_of[4], (POINTS,), jnp.float32, math.log(0.04), math.log(0.4))), 0.04, 0.4)
    return {"fields": fields, "evaluate": evaluate, "project": project, "feed": feed, "kill": kill}


TIME_STEP = 0.5
DIFFUSION = (1.0, 0.5)


def reaction_row(row_fields, evaluate, project, feed, kill):
    at_points = jnp.einsum("qm,fmc->fqc", evaluate.astype(jnp.float32), row_fields.astype(jnp.float32))
    u_val = at_points[0]
    v_val = at_points[1]
    feed_col = feed[:, None]
    kill_col = kill[:, None]
    squared = u_val * v_val * v_val
    reacted = jnp.stack([-squared + feed_col * (1.0 - u_val), squared - (feed_col + kill_col) * v_val]).astype(jnp.bfloat16)
    return jnp.einsum("mq,fqc->fmc", project.astype(jnp.float32), reacted.astype(jnp.float32))


def reference(fields, evaluate, project, feed, kill):
    rounded = fields.astype(jnp.bfloat16)
    rows_first = jnp.moveaxis(rounded, 2, 0)
    projected = lax.map(lambda row_fields: reaction_row(row_fields, evaluate, project, feed, kill), rows_first)
    projected = jnp.moveaxis(projected, 0, 2)
    right_side = fields + TIME_STEP * projected
    weights = jnp.array(DIFFUSION, jnp.float32).reshape(2, 1, 1, 1)
    iterate = right_side
    for sweep_index in range(SWEEPS):
        padded = jnp.pad(iterate, ((0, 0), (0, 0), (1, 1), (0, 0)))
        neighbours = jnp.roll(iterate, 1, 3) + jnp.roll(iterate, -1, 3) + padded[:, :, 2:, :] + padded[:, :, :-2, :]
        iterate = (right_side + weights * neighbours) / (1.0 + 4.0 * weights)
    return iterate
```

```python
import jax
import jax.numpy as jnp
from jax import lax
from jax.experimental import pallas as pl
from jax.experimental.pallas import tpu as pltpu
from jax.sharding import PartitionSpec as P

MESH = pl.DeviceIdType.MESH
F32, BF16 = jnp.float32, jnp.bfloat16

SWEEPS = 4
TIME_STEP = 0.5
DIFFUSION = (1.0, 0.5)

MODES, POINTS = 288, 1584
PARTS = 8
LOCAL = 36
ROWS, COLS = 64, 256
CHUNKS = 4
TILES = 9
MESSAGE = 144
DEPTH = 384
PADDED = 1664
BLOCK = 528
OUT_ROWS = 320
GROUPS = ((0, 3), (3, 6), (6, 9))
PARTNERS = ((0, 1), (1, 0), (3, 0), (2, 0), (1, 1), (3, 1), (2, 1))


def iota(shape, dim):
    return lax.broadcasted_iota(jnp.int32, shape, dim)


def kernel(
    fields, evaluate, project, rates, out,
    fv, ft, ita, itb, ev, pj, weights, proj, rate_b,
    snd, rcv, reacted, bsnd, brcv, hsnd, hrcv,
    in_sem, table_sem, out_sem, own_sem, fs_sem, fr_sem, bown_sem, bs_sem, br_sem, hs_sem, hr_sem,
):
    me, col = lax.axis_index("mode"), lax.axis_index("col")
    cols = lax.axis_size("col")
    right, left = (col + 1) % cols, (col + cols - 1) % cols
    partners = [((me // 2 + dy) % 4) * 2 + (me % 2 + dx) % 2 for dy, dx in PARTNERS]

    barrier = pltpu.get_barrier_semaphore()
    for part in partners:
        pl.semaphore_signal(barrier, inc=1, device_id=(part, col), device_id_type=MESH)
    for side in (right, left):
        pl.semaphore_signal(barrier, inc=1, device_id=(me, side), device_id_type=MESH)

    planes = fv.reshape(2, 2 * LOCAL, ROWS, 128)

    def load(chunk, half):
        rows = pl.ds(16 * chunk, 16)
        return pltpu.make_async_copy(
            fields.at[:, rows, pl.ds(128 * half, 128)], planes.at[half, :, rows, :], in_sem.at[chunk, half]
        )

    for chunk in range(CHUNKS):
        for half in range(2):
            load(chunk, half).start()
    tables = [
        pltpu.make_async_copy(evaluate, ev, table_sem.at[0]),
        pltpu.make_async_copy(project, pj, table_sem.at[1]),
    ]
    for table in tables:
        table.start()

    def prepare(chunk):
        def one(dest, carry):
            row = 16 * chunk + 2 * dest
            values = []
            for j in range(2):
                values.append([])
                for g in range(TILES):
                    rows = pl.ds(8 * g * ROWS + row + j, 8, stride=ROWS)
                    values[j].append(jnp.concatenate([fv[0, rows, :], fv[1, rows, :]], axis=1))
                for g in range(TILES):
                    ft[g, row + j + 1, :, :COLS] = values[j][g]
            for j in range(2):
                for k, g in enumerate((0, 2, 5, 7)):
                    pair = jnp.concatenate([values[j][g], values[j][g + 1]], axis=0)
                    snd[dest, chunk, 64 * j + 16 * k : 64 * j + 16 * k + 16, :] = pair.astype(BF16)
            pair = jnp.concatenate([values[0][4], values[1][4]], axis=0)
            snd[dest, chunk, 128:144, :] = pair.astype(BF16)
            return carry

        lax.fori_loop(0, PARTS, one, 0)

    def forward(chunk, k):
        part = partners[k]
        return pltpu.make_async_remote_copy(
            src_ref=snd.at[part, chunk], dst_ref=rcv.at[chunk, me],
            send_sem=fs_sem.at[chunk, k], recv_sem=fr_sem.at[chunk, me],
            device_id=(part, col), device_id_type=MESH,
        )

    def forward_in(chunk, k):
        part = partners[k]
        return pltpu.make_async_remote_copy(
            src_ref=snd.at[part, chunk], dst_ref=rcv.at[chunk, part],
            send_sem=fs_sem.at[chunk, k], recv_sem=fr_sem.at[chunk, part],
            device_id=(part, col), device_id_type=MESH,
        )

    def own(chunk):
        return pltpu.make_async_copy(snd.at[me, chunk], rcv.at[chunk, me], own_sem.at[chunk])

    for half in range(2):
        load(0, half).wait()
    prepare(0)
    pl.semaphore_wait(barrier, len(PARTNERS) + 2)
    for chunk in range(CHUNKS):
        if chunk > 0:
            for half in range(2):
                load(chunk, half).wait()
            prepare(chunk)
        for k in range(len(PARTNERS)):
            forward(chunk, k).start()
        own(chunk).start()

    for g in range(TILES):
        ft[g, 0, :, :] = jnp.zeros((8, DEPTH), F32)
        ft[g, ROWS + 1, :, :] = jnp.zeros((8, DEPTH), F32)
    for ref in (ita, itb):
        ref[0, :, :] = jnp.zeros((8, DEPTH), F32)
        ref[ROWS + 1, :, :] = jnp.zeros((8, DEPTH), F32)
    for table in tables:
        table.wait()
    mode = iota((MODES, DEPTH), 0)
    slot = iota((MODES, DEPTH), 1)
    mixed = slot - 256
    for f in range(2):
        main_mode = LOCAL * (slot >> 5) + (slot & 31) + 4 * f
        place = mixed & 7
        mix_mode = LOCAL * (mixed >> 4) + (place - 4 if f else place + 32)
        for j in range(2):
            mine = (((mixed >> 3) & 1) == j) & ((place >= 4) if f else (place < 4))
            want = jnp.where(slot < 256, main_mode, jnp.where(mine, mix_mode, -1))
            onehot = jnp.where(want == mode, 1.0, 0.0).astype(BF16)
            weights[2 * f + j] = jnp.dot(ev[...], onehot, preferred_element_type=F32).astype(BF16)
    mode = iota((OUT_ROWS, MODES), 1)
    slot = iota((OUT_ROWS, MODES), 0)
    mixed = slot - 256
    for f in range(2):
        main_mode = LOCAL * (slot >> 5) + (slot & 31) + 4 * f
        place = mixed & 7
        mix_mode = LOCAL * (mixed >> 3) + (place - 4 if f else place + 32)
        mine = (place >= 4) if f else (place < 4)
        want = jnp.where(slot < 256, main_mode, jnp.where(mine, mix_mode, -1))
        onehot = jnp.where(want == mode, 1.0, 0.0).astype(BF16)
        proj[f, :, 1536:] = jnp.zeros((OUT_ROWS, 128), BF16)
        proj[f, :, :POINTS] = jnp.dot(onehot, pj[...], preferred_element_type=F32).astype(BF16)
        reacted[f, POINTS:, :] = jnp.zeros((PADDED - POINTS, 2 * COLS), BF16)
    eye = iota((128, 128), 0) == iota((128, 128), 1)
    for q in range(0, POINTS, 128):
        count = min(128, POINTS - q)
        for f in range(2):
            spread = jnp.broadcast_to(rates[f : f + 1, q : q + 128], (128, 128))
            column = jnp.sum(jnp.where(eye, spread, 0.0), axis=1, keepdims=True)
            rate_b[f, q : q + count, :] = jnp.broadcast_to(column[:count], (count, 128))

    def react(chunk):
        for k in range(len(PARTNERS)):
            forward_in(chunk, k).wait_recv()
        own(chunk).wait()

        def block(b, carry):
            rows = pl.ds(pl.multiple_of(b * BLOCK, 16), BLOCK)
            feed = jnp.tile(rate_b[0, rows, :], (1, 2))
            loss = jnp.tile(rate_b[1, rows, :], (1, 2))
            for j in range(2):
                mix = rcv[chunk, :, 128:144, :].reshape(128, COLS)
                ub = jnp.concatenate([rcv[chunk, :, 64 * j : 64 * j + 32, :].reshape(256, COLS), mix], axis=0)
                vb = jnp.concatenate([rcv[chunk, :, 64 * j + 32 : 64 * j + 64, :].reshape(256, COLS), mix], axis=0)
                u = jnp.dot(weights[j, rows, :], ub, preferred_element_type=F32)
                v = jnp.dot(weights[2 + j, rows, :], vb, preferred_element_type=F32)
                squared = u * v * v
                lanes = slice(COLS * j, COLS * j + COLS)
                reacted[0, rows, lanes] = (feed * (1.0 - u) - squared).astype(BF16)
                reacted[1, rows, lanes] = (squared - loss * v).astype(BF16)
            return carry

        lax.fori_loop(0, POINTS // BLOCK, block, 0)

    def project_back(chunk):
        mix = None
        for f in range(2):
            total = jnp.dot(proj[f], reacted[f], preferred_element_type=F32)
            main = jnp.stack(
                [total[:256, :COLS].reshape(32, 8, COLS), total[:256, COLS:].reshape(32, 8, COLS)], axis=1
            ).astype(BF16)
            bsnd[:, 5 * f : 5 * f + 4, chunk] = main.reshape(PARTS, 4, 16, COLS)
            mix = total[256:] if f == 0 else mix + total[256:]
        mix = jnp.stack([mix[:, :COLS].reshape(8, 8, COLS), mix[:, COLS:].reshape(8, 8, COLS)], axis=1)
        bsnd[:, 4, chunk] = mix.astype(BF16).reshape(PARTS, 16, COLS)

    def part_of(item, row):
        first, last = GROUPS[max(0, item - 3)]
        if item < CHUNKS:
            return row[0].at[row[1], first:last, item]
        return row[0].at[row[1], first:last]

    def backward(item, k, incoming=False):
        part = partners[k]
        slot = part if incoming else me
        return pltpu.make_async_remote_copy(
            src_ref=part_of(item, (bsnd, part)), dst_ref=part_of(item, (brcv, slot)),
            send_sem=bs_sem.at[item, k], recv_sem=br_sem.at[item, slot],
            device_id=(part, col), device_id_type=MESH,
        )

    def back_own(item):
        return pltpu.make_async_copy(part_of(item, (bsnd, me)), part_of(item, (brcv, me)), bown_sem.at[item])

    def send_back(item):
        for k in range(len(PARTNERS)):
            backward(item, k).start()
        back_own(item).start()

    items = CHUNKS + len(GROUPS) - 1
    for chunk in range(CHUNKS):
        react(chunk)
        project_back(chunk)
        send_back(chunk)
    for item in range(CHUNKS, items):
        send_back(item)

    lane = iota((8, 128), 1)

    def gather(index):
        first, last = GROUPS[index]
        for item in range(CHUNKS) if index == 0 else (CHUNKS + index - 1,):
            for k in range(len(PARTNERS)):
                backward(item, k, True).wait_recv()
            back_own(item).wait()

        def tile(g, carry):
            def rows16(c, carry):
                packed = jnp.zeros((8, 128), F32)
                for s in range(PARTS):
                    pair = brcv[s, g, c].astype(F32)
                    for j in range(2):
                        row = 16 * c + 2 * s + j + 1
                        value = ft[g, row, :, :COLS] + TIME_STEP * pair[8 * j : 8 * j + 8]
                        ft[g, row, :, :COLS] = value
                        edge = jnp.where(lane < 64, value[:, :128], value[:, 128:])
                        at = 2 * s + j
                        packed = jnp.where((lane >> 3) == at, pltpu.roll(edge, (8 * at + 4) % 128, 1), packed)
                hsnd[g, c] = packed
                return carry

            return lax.fori_loop(0, CHUNKS, rows16, carry)

        lax.fori_loop(first, last, tile, 0)

    def halo(index, side, incoming=False):
        first, last = GROUPS[index]
        there = 1 - side if incoming else side
        return pltpu.make_async_remote_copy(
            src_ref=hsnd.at[first:last], dst_ref=hrcv.at[there, first:last],
            send_sem=hs_sem.at[index, side], recv_sem=hr_sem.at[index, there],
            device_id=(me, left if side else right), device_id_type=MESH,
        )

    def sweeps(index):
        first, last = GROUPS[index]
        for side in range(2):
            halo(index, side, True).wait_recv()

        def tile(g, carry):
            pair = 8 * g + iota((8, DEPTH), 0)
            weight = jnp.where(pair < LOCAL, DIFFUSION[0], DIFFUSION[1])
            keep = jnp.broadcast_to((1.0 / (1.0 + 4.0 * weight))[None], (8, 8, DEPTH)).reshape(64, DEPTH)
            near = jnp.broadcast_to((weight / (1.0 + 4.0 * weight))[None], (8, 8, DEPTH)).reshape(64, DEPTH)

            def widen(c, carry):
                both = jnp.where((lane & 7) < 4, hrcv[0, g, c], hrcv[1, g, c])
                for at in range(16):
                    ft[g, 16 * c + at + 1, :, COLS:] = pltpu.roll(both, (124 - 8 * at) % 128, 1)
                return carry

            lax.fori_loop(0, CHUNKS, widen, 0)

            def sweep(source, store):
                def rows8(b, carry):
                    start = 8 * b
                    window = source(pl.ds(start, 10))
                    middle = window[1:9].reshape(64, DEPTH)
                    total = (window[0:8] + window[2:10]).reshape(64, DEPTH)
                    total = total + (pltpu.roll(middle, 1, 1) + pltpu.roll(middle, DEPTH - 1, 1))
                    base = ft[g, pl.ds(start + 1, 8)].reshape(64, DEPTH)
                    store(start, (keep * base + near * total).reshape(8, 8, DEPTH))
                    return carry

                lax.fori_loop(0, ROWS // 8, rows8, 0)

            def into(ref):
                def store(start, value):
                    ref[pl.ds(start + 1, 8)] = value

                return store

            def last_store(start, value):
                for i in range(8):
                    rows = pl.ds(8 * g * ROWS + start + i, 8, stride=ROWS)
                    fv[0, rows, :] = value[i, :, :128]
                    fv[1, rows, :] = value[i, :, 128:COLS]

            sweep(lambda rows: ft[g, rows], into(ita))
            sweep(lambda rows: ita[rows], into(itb))
            sweep(lambda rows: itb[rows], into(ita))
            sweep(lambda rows: ita[rows], last_store)
            return carry

        lax.fori_loop(first, last, tile, 0)

    def write(index, half):
        first, last = GROUPS[index]
        rows = pl.ds(8 * first, 8 * (last - first))
        return pltpu.make_async_copy(
            planes.at[half, rows], out.at[rows, :, pl.ds(128 * half, 128)], out_sem.at[index, half]
        )

    count = len(GROUPS)
    for index in range(count + 1):
        if index < count:
            gather(index)
            for side in range(2):
                halo(index, side).start()
        if index > 0:
            sweeps(index - 1)
            for half in range(2):
                write(index - 1, half).start()

    for chunk in range(CHUNKS):
        for k in range(len(PARTNERS)):
            forward(chunk, k).wait_send()
    for item in range(items):
        for k in range(len(PARTNERS)):
            backward(item, k).wait_send()
    for index in range(count):
        for side in range(2):
            halo(index, side).wait_send()
            write(index, side).wait()


def body(fields, evaluate, project, feed, kill):
    rates = jnp.pad(jnp.stack([feed, feed + kill]), ((0, 0), (0, PADDED - POINTS)))
    items = CHUNKS + len(GROUPS) - 1
    partners = len(PARTNERS)
    anywhere = pl.BlockSpec(memory_space=pl.ANY)
    dma = pltpu.SemaphoreType.DMA
    stepped = pl.pallas_call(
        kernel,
        out_shape=jax.ShapeDtypeStruct((2 * LOCAL, ROWS, COLS), F32),
        in_specs=[anywhere, anywhere, anywhere, pl.BlockSpec(memory_space=pltpu.VMEM)],
        out_specs=anywhere,
        scratch_shapes=[
            pltpu.VMEM((2, 2 * LOCAL * ROWS, 128), F32),
            pltpu.VMEM((TILES, ROWS + 2, 8, DEPTH), F32),
            pltpu.VMEM((ROWS + 2, 8, DEPTH), F32),
            pltpu.VMEM((ROWS + 2, 8, DEPTH), F32),
            pltpu.VMEM((POINTS, MODES), BF16),
            pltpu.VMEM((MODES, POINTS), BF16),
            pltpu.VMEM((4, POINTS, DEPTH), BF16),
            pltpu.VMEM((2, OUT_ROWS, PADDED), BF16),
            pltpu.VMEM((2, POINTS, 128), F32),
            pltpu.VMEM((PARTS, CHUNKS, MESSAGE, COLS), BF16),
            pltpu.VMEM((CHUNKS, PARTS, MESSAGE, COLS), BF16),
            pltpu.VMEM((2, PADDED, 2 * COLS), BF16),
            pltpu.VMEM((PARTS, TILES, CHUNKS, 16, COLS), BF16),
            pltpu.VMEM((PARTS, TILES, CHUNKS, 16, COLS), BF16),
            pltpu.VMEM((TILES, CHUNKS, 8, 128), F32),
            pltpu.VMEM((2, TILES, CHUNKS, 8, 128), F32),
            dma((CHUNKS, 2)),
            dma((2,)),
            dma((len(GROUPS), 2)),
            dma((CHUNKS,)),
            dma((CHUNKS, partners)),
            dma((CHUNKS, PARTS)),
            dma((items,)),
            dma((items, partners)),
            dma((items, PARTS)),
            dma((len(GROUPS), 2)),
            dma((len(GROUPS), 2)),
        ],
        compiler_params=pltpu.CompilerParams(
            collective_id=0, has_side_effects=True, vmem_limit_bytes=60 * 2**20
        ),
        cost_estimate=pl.CostEstimate(
            flops=8 * 2 * LOCAL * ROWS * COLS * POINTS // 2, bytes_accessed=12 * 2**20, transcendentals=0
        ),
    )(fields.reshape(2 * LOCAL, ROWS, COLS), evaluate, project, rates)
    return stepped.reshape(2, LOCAL, ROWS, COLS)


def solution(mesh):
    in_specs = (P(None, "mode", None, "col"), P(), P(), P(), P())
    out_specs = P(None, "mode", None, "col")
    return jax.shard_map(body, mesh=mesh, in_specs=in_specs, out_specs=out_specs, check_vma=False)
```

```python
import jax
import jax.numpy as jnp
from jax import lax
from jax.experimental import pallas as pl
from jax.experimental.pallas import tpu as pltpu
from jax.sharding import PartitionSpec as P

MESH = pl.DeviceIdType.MESH
F32, BF16 = jnp.float32, jnp.bfloat16

VMEM_LIMIT = 58 * 2**20
TIME_STEP = 0.5
DIFFUSION = (1.0, 0.5)

MODES, POINTS = 288, 1584
PARTS = 8
LOCAL = 36
ROWS, COLS = 64, 256
CHUNKS = 4
TILES = 9
MESSAGE = 144
DEPTH = 384
PADDED = 1664
BLOCK = 528
OUT_ROWS = 320
GROUPS = ((0, 2), (2, 4), (4, 6), (6, 8), (8, 9))
PARTNERS = ((0, 1), (1, 0), (3, 0), (2, 0), (1, 1), (3, 1), (2, 1))


def iota(shape, dim):
    return lax.broadcasted_iota(jnp.int32, shape, dim)


def kernel(
    fields, evaluate, project, feed, kill, out,
    fv, ft, ita, itb, ev, pj, weights, proj, rate_b,
    snd, rcv, reacted, bsnd, brcv, hsnd, hrcv,
    in_sem, table_sem, out_sem, own_sem, fs_sem, fr_sem, bown_sem, bs_sem, br_sem, hs_sem, hr_sem,
):
    me, col = lax.axis_index("mode"), lax.axis_index("col")
    cols = lax.axis_size("col")
    right, left = (col + 1) % cols, (col + cols - 1) % cols
    partners = [((me // 2 + dy) % 4) * 2 + (me % 2 + dx) % 2 for dy, dx in PARTNERS]

    barrier = pltpu.get_barrier_semaphore()
    for part in partners:
        pl.semaphore_signal(barrier, inc=1, device_id=(part, col), device_id_type=MESH)
    for side in (right, left):
        pl.semaphore_signal(barrier, inc=1, device_id=(me, side), device_id_type=MESH)

    planes = fv.reshape(2, 2 * LOCAL, ROWS, 128)

    def load(chunk, half):
        rows = pl.ds(16 * chunk, 16)
        return pltpu.make_async_copy(
            fields.at[:, rows, pl.ds(128 * half, 128)], planes.at[half, :, rows, :], in_sem.at[chunk, half]
        )

    for chunk in range(CHUNKS):
        for half in range(2):
            load(chunk, half).start()
    tables = [
        pltpu.make_async_copy(evaluate, ev, table_sem.at[0]),
        pltpu.make_async_copy(project, pj, table_sem.at[1]),
    ]
    for table in tables:
        table.start()

    def prepare(chunk):
        def one(dest, carry):
            row = 16 * chunk + 2 * dest
            values = []
            for j in range(2):
                values.append([])
                for g in range(TILES):
                    rows = pl.ds(8 * g * ROWS + row + j, 8, stride=ROWS)
                    values[j].append(jnp.concatenate([fv[0, rows, :], fv[1, rows, :]], axis=1))
                for g in range(TILES):
                    ft[g, row + j + 1, :, :COLS] = values[j][g]
            for j in range(2):
                for k, g in enumerate((0, 2, 5, 7)):
                    pair = jnp.concatenate([values[j][g], values[j][g + 1]], axis=0)
                    snd[dest, chunk, 64 * j + 16 * k : 64 * j + 16 * k + 16, :] = pair.astype(BF16)
            pair = jnp.concatenate([values[0][4], values[1][4]], axis=0)
            snd[dest, chunk, 128:144, :] = pair.astype(BF16)
            return carry

        lax.fori_loop(0, PARTS, one, 0)

    def forward(chunk, k):
        part = partners[k]
        return pltpu.make_async_remote_copy(
            src_ref=snd.at[part, chunk], dst_ref=rcv.at[chunk, me],
            send_sem=fs_sem.at[chunk, k], recv_sem=fr_sem.at[chunk, me],
            device_id=(part, col), device_id_type=MESH,
        )

    def forward_in(chunk, k):
        part = partners[k]
        return pltpu.make_async_remote_copy(
            src_ref=snd.at[part, chunk], dst_ref=rcv.at[chunk, part],
            send_sem=fs_sem.at[chunk, k], recv_sem=fr_sem.at[chunk, part],
            device_id=(part, col), device_id_type=MESH,
        )

    def own(chunk):
        return pltpu.make_async_copy(snd.at[me, chunk], rcv.at[chunk, me], own_sem.at[chunk])

    for half in range(2):
        load(0, half).wait()
    prepare(0)
    pl.semaphore_wait(barrier, len(PARTNERS) + 2)
    for chunk in range(CHUNKS):
        if chunk > 0:
            for half in range(2):
                load(chunk, half).wait()
            prepare(chunk)
        for k in range(len(PARTNERS)):
            forward(chunk, k).start()
        own(chunk).start()

    for g in range(TILES):
        ft[g, 0, :, :] = jnp.zeros((8, DEPTH), F32)
        ft[g, ROWS + 1, :, :] = jnp.zeros((8, DEPTH), F32)
    for ref in (ita, itb):
        ref[0, :, :] = jnp.zeros((8, DEPTH), F32)
        ref[ROWS + 1, :, :] = jnp.zeros((8, DEPTH), F32)
    for table in tables:
        table.wait()
    mode = iota((MODES, DEPTH), 0)
    slot = iota((MODES, DEPTH), 1)
    mixed = slot - 256
    for f in range(2):
        main_mode = LOCAL * (slot >> 5) + (slot & 31) + 4 * f
        place = mixed & 7
        mix_mode = LOCAL * (mixed >> 4) + (place - 4 if f else place + 32)
        for j in range(2):
            mine = (((mixed >> 3) & 1) == j) & ((place >= 4) if f else (place < 4))
            want = jnp.where(slot < 256, main_mode, jnp.where(mine, mix_mode, -1))
            onehot = jnp.where(want == mode, 1.0, 0.0).astype(BF16)
            weights[2 * f + j] = lax.dot_general(
                ev[...], onehot, (((0,), (0,)), ((), ())), preferred_element_type=F32
            ).astype(BF16)
    mode = iota((OUT_ROWS, MODES), 1)
    slot = iota((OUT_ROWS, MODES), 0)
    mixed = slot - 256
    for f in range(2):
        main_mode = LOCAL * (slot >> 5) + (slot & 31) + 4 * f
        place = mixed & 7
        mix_mode = LOCAL * (mixed >> 3) + (place - 4 if f else place + 32)
        mine = (place >= 4) if f else (place < 4)
        want = jnp.where(slot < 256, main_mode, jnp.where(mine, mix_mode, -1))
        onehot = jnp.where(want == mode, 1.0, 0.0).astype(BF16)
        proj[f, :, 1536:] = jnp.zeros((OUT_ROWS, 128), BF16)
        proj[f, :, :POINTS] = jnp.dot(onehot, pj[...], preferred_element_type=F32).astype(BF16)
        reacted[f, POINTS:, :] = jnp.zeros((PADDED - POINTS, 2 * COLS), BF16)
    eye = iota((128, 128), 0) == iota((128, 128), 1)
    for q in (*range(0, POINTS - 128, 128), POINTS - 128):
        supply = feed[q : q + 128].reshape(1, 128)
        for f, rate in enumerate((supply, supply + kill[q : q + 128].reshape(1, 128))):
            column = jnp.sum(jnp.where(eye, jnp.broadcast_to(rate, (128, 128)), 0.0), axis=1, keepdims=True)
            rate_b[f, q : q + 128, :] = jnp.broadcast_to(column, (128, 128))

    def react(chunk):
        for k in range(len(PARTNERS)):
            forward_in(chunk, k).wait_recv()
        own(chunk).wait()

        def block(b, carry):
            rows = pl.ds(pl.multiple_of(b * BLOCK, 16), BLOCK)
            feed = jnp.tile(rate_b[0, rows, :], (1, 2))
            loss = jnp.tile(rate_b[1, rows, :], (1, 2))
            for j in range(2):
                mix = rcv[chunk, :, 128:144, :].reshape(128, COLS)
                ub = jnp.concatenate([rcv[chunk, :, 64 * j : 64 * j + 32, :].reshape(256, COLS), mix], axis=0)
                vb = jnp.concatenate([rcv[chunk, :, 64 * j + 32 : 64 * j + 64, :].reshape(256, COLS), mix], axis=0)
                u = jnp.dot(weights[j, rows, :], ub, preferred_element_type=F32)
                v = jnp.dot(weights[2 + j, rows, :], vb, preferred_element_type=F32)
                squared = u * v * v
                lanes = slice(COLS * j, COLS * j + COLS)
                reacted[0, rows, lanes] = (feed * (1.0 - u) - squared).astype(BF16)
                reacted[1, rows, lanes] = (squared - loss * v).astype(BF16)
            return carry

        lax.fori_loop(0, POINTS // BLOCK, block, 0)

    def project_back(chunk):
        mix = None
        for f in range(2):
            total = jnp.dot(proj[f], reacted[f], preferred_element_type=F32)
            main = jnp.stack(
                [total[:256, :COLS].reshape(32, 8, COLS), total[:256, COLS:].reshape(32, 8, COLS)], axis=1
            ).astype(BF16)
            bsnd[:, 5 * f : 5 * f + 4, chunk] = main.reshape(PARTS, 4, 16, COLS)
            mix = total[256:] if f == 0 else mix + total[256:]
        mix = jnp.stack([mix[:, :COLS].reshape(8, 8, COLS), mix[:, COLS:].reshape(8, 8, COLS)], axis=1)
        bsnd[:, 4, chunk] = mix.astype(BF16).reshape(PARTS, 16, COLS)

    def part_of(item, row):
        first, last = GROUPS[max(0, item - 3)]
        if item < CHUNKS:
            return row[0].at[row[1], first:last, item]
        return row[0].at[row[1], first:last]

    def backward(item, k, incoming=False):
        part = partners[k]
        slot = part if incoming else me
        return pltpu.make_async_remote_copy(
            src_ref=part_of(item, (bsnd, part)), dst_ref=part_of(item, (brcv, slot)),
            send_sem=bs_sem.at[item, k], recv_sem=br_sem.at[item, slot],
            device_id=(part, col), device_id_type=MESH,
        )

    def back_own(item):
        return pltpu.make_async_copy(part_of(item, (bsnd, me)), part_of(item, (brcv, me)), bown_sem.at[item])

    def send_back(item):
        for k in range(len(PARTNERS)):
            backward(item, k).start()
        back_own(item).start()

    items = CHUNKS + len(GROUPS) - 1
    for chunk in range(CHUNKS):
        react(chunk)
        project_back(chunk)
        send_back(chunk)
    send_back(CHUNKS)

    lane = iota((8, 128), 1)

    def gather(index):
        first, last = GROUPS[index]
        for item in range(CHUNKS) if index == 0 else (CHUNKS + index - 1,):
            for k in range(len(PARTNERS)):
                backward(item, k, True).wait_recv()
            back_own(item).wait()
        if index + 2 < len(GROUPS):
            send_back(CHUNKS + index + 1)

        def tile(g, carry):
            def rows16(c, carry):
                packed = jnp.zeros((8, 128), F32)
                for s in range(PARTS):
                    pair = brcv[s, g, c].astype(F32)
                    for j in range(2):
                        row = 16 * c + 2 * s + j + 1
                        value = ft[g, row, :, :COLS] + TIME_STEP * pair[8 * j : 8 * j + 8]
                        ft[g, row, :, :COLS] = value
                        edge = jnp.where(lane < 64, value[:, :128], value[:, 128:])
                        at = 2 * s + j
                        packed = jnp.where((lane >> 3) == at, pltpu.roll(edge, (8 * at + 4) % 128, 1), packed)
                hsnd[g, c] = packed
                return carry

            return lax.fori_loop(0, CHUNKS, rows16, carry)

        lax.fori_loop(first, last, tile, 0)

    def halo(index, side, incoming=False):
        first, last = GROUPS[index]
        there = 1 - side if incoming else side
        return pltpu.make_async_remote_copy(
            src_ref=hsnd.at[first:last], dst_ref=hrcv.at[there, first:last],
            send_sem=hs_sem.at[index, side], recv_sem=hr_sem.at[index, there],
            device_id=(me, left if side else right), device_id_type=MESH,
        )

    def sweeps(index):
        first, last = GROUPS[index]
        for side in range(2):
            halo(index, side, True).wait_recv()

        def tile(g, carry):
            pair = 8 * g + iota((8, 128), 0)
            weight = jnp.where(pair < LOCAL, DIFFUSION[0], DIFFUSION[1])
            keep = 1.0 / (1.0 + 4.0 * weight)
            near = weight / (1.0 + 4.0 * weight)

            def widen(c, carry):
                both = jnp.where((lane & 7) < 4, hrcv[0, g, c], hrcv[1, g, c])
                for at in range(16):
                    ft[g, 16 * c + at + 1, :, COLS:] = pltpu.roll(both, (124 - 8 * at) % 128, 1)
                return carry

            lax.fori_loop(0, CHUNKS, widen, 0)

            def row(ref, r):
                return [ref[r, :, 128 * t : 128 * t + 128] for t in range(3)]

            def sweep(source, store, count):
                up, middle = row(source, 0), row(source, 1)
                for r in range(1, ROWS + 1):
                    down = row(source, r + 1)
                    base = row(ft.at[g], r)
                    after = [pltpu.roll(t, 1, 1) for t in middle]
                    before = [pltpu.roll(t, 127, 1) for t in middle]
                    result = []
                    for t in range(count):
                        sides = jnp.where(lane == 0, after[(t + 2) % 3], after[t])
                        sides = sides + jnp.where(lane == 127, before[(t + 1) % 3], before[t])
                        result.append(keep * base[t] + near * ((up[t] + down[t]) + sides))
                    store(r, result)
                    up, middle = middle, down

            def into(ref):
                def store(r, result):
                    for t in range(3):
                        ref[r, :, 128 * t : 128 * t + 128] = result[t]

                return store

            def last_store(r, result):
                rows = pl.ds(8 * g * ROWS + r - 1, 8, stride=ROWS)
                fv[0, rows, :] = result[0]
                fv[1, rows, :] = result[1]

            sweep(ft.at[g], into(ita), 3)
            sweep(ita, into(itb), 3)
            sweep(itb, into(ita), 3)
            sweep(ita, last_store, 2)
            return carry

        lax.fori_loop(first, last, tile, 0)

    def write(index, half):
        first, last = GROUPS[index]
        rows = pl.ds(8 * first, 8 * (last - first))
        return pltpu.make_async_copy(
            planes.at[half, rows], out.at[rows, :, pl.ds(128 * half, 128)], out_sem.at[index, half]
        )

    count = len(GROUPS)
    for index in range(count + 1):
        if index < count:
            gather(index)
            for side in range(2):
                halo(index, side).start()
        if index > 0:
            sweeps(index - 1)
            for half in range(2):
                write(index - 1, half).start()

    for chunk in range(CHUNKS):
        for k in range(len(PARTNERS)):
            forward(chunk, k).wait_send()
    for item in range(items):
        for k in range(len(PARTNERS)):
            backward(item, k).wait_send()
    for index in range(count):
        for side in range(2):
            halo(index, side).wait_send()
            write(index, side).wait()


def body(fields, evaluate, project, feed, kill):
    items = CHUNKS + len(GROUPS) - 1
    partners = len(PARTNERS)
    hbm = pl.BlockSpec(memory_space=pltpu.MemorySpace.HBM)
    vmem = pl.BlockSpec(memory_space=pltpu.VMEM)
    dma = pltpu.SemaphoreType.DMA
    stepped = pl.pallas_call(
        kernel,
        out_shape=jax.ShapeDtypeStruct((2 * LOCAL, ROWS, COLS), F32),
        in_specs=[hbm, hbm, hbm, vmem, vmem],
        out_specs=pl.BlockSpec(memory_space=pl.ANY),
        scratch_shapes=[
            pltpu.VMEM((2, 2 * LOCAL * ROWS, 128), F32),
            pltpu.VMEM((TILES, ROWS + 2, 8, DEPTH), F32),
            pltpu.VMEM((ROWS + 2, 8, DEPTH), F32),
            pltpu.VMEM((ROWS + 2, 8, DEPTH), F32),
            pltpu.VMEM((MODES, POINTS), BF16),
            pltpu.VMEM((MODES, POINTS), BF16),
            pltpu.VMEM((4, POINTS, DEPTH), BF16),
            pltpu.VMEM((2, OUT_ROWS, PADDED), BF16),
            pltpu.VMEM((2, POINTS, 128), F32),
            pltpu.VMEM((PARTS, CHUNKS, MESSAGE, COLS), BF16),
            pltpu.VMEM((CHUNKS, PARTS, MESSAGE, COLS), BF16),
            pltpu.VMEM((2, PADDED, 2 * COLS), BF16),
            pltpu.VMEM((PARTS, TILES, CHUNKS, 16, COLS), BF16),
            pltpu.VMEM((PARTS, TILES, CHUNKS, 16, COLS), BF16),
            pltpu.VMEM((TILES, CHUNKS, 8, 128), F32),
            pltpu.VMEM((2, TILES, CHUNKS, 8, 128), F32),
            dma((CHUNKS, 2)),
            dma((2,)),
            dma((len(GROUPS), 2)),
            dma((CHUNKS,)),
            dma((CHUNKS, partners)),
            dma((CHUNKS, PARTS)),
            dma((items,)),
            dma((items, partners)),
            dma((items, PARTS)),
            dma((len(GROUPS), 2)),
            dma((len(GROUPS), 2)),
        ],
        compiler_params=pltpu.CompilerParams(
            collective_id=0, has_side_effects=True, vmem_limit_bytes=VMEM_LIMIT
        ),
        cost_estimate=pl.CostEstimate(
            flops=8 * 2 * LOCAL * ROWS * COLS * POINTS // 2, bytes_accessed=12 * 2**20, transcendentals=0
        ),
    )(fields.reshape(2 * LOCAL, ROWS, COLS), evaluate.T, project, feed, kill)
    return stepped.reshape(2, LOCAL, ROWS, COLS)


def solution(mesh):
    in_specs = (P(None, "mode", None, "col"), P(), P(), P(), P())
    out_specs = P(None, "mode", None, "col")
    return jax.shard_map(body, mesh=mesh, in_specs=in_specs, out_specs=out_specs, check_vma=False)
```

```python
import jax
import jax.numpy as jnp
from jax import lax
from jax.experimental import pallas as pl
from jax.experimental.pallas import tpu as pltpu
from jax.sharding import PartitionSpec as P

MESH = pl.DeviceIdType.MESH
F32, BF16 = jnp.float32, jnp.bfloat16

VMEM_LIMIT = 58 * 2**20
TIME_STEP = 0.5
DIFFUSION = (1.0, 0.5)

MODES, POINTS = 288, 1584
PARTS = 8
LOCAL = 36
ROWS, COLS = 64, 256
CHUNKS = 4
TILES = 9
MESSAGE = 144
DEPTH = 384
PADDED = 1664
BLOCK = 528
OUT_ROWS = 320
WINDOW = 3
LAG = 2
EARLY = 2
PARTNERS = ((0, 1), (1, 0), (3, 0), (2, 0), (1, 1), (3, 1), (2, 1))


def iota(shape, dim):
    return lax.broadcasted_iota(jnp.int32, shape, dim)


def kernel(
    fields, evaluate, project, feed, kill, out,
    fv, ft, ita, itb, ev, pj, weights, proj, rate_b,
    snd, rcv, reacted, bsnd, brcv, hsnd, hrcv,
    in_sem, table_sem, out_sem, own_sem, fs_sem, fr_sem, bown_sem, bs_sem, br_sem, hs_sem, hr_sem,
):
    me, col = lax.axis_index("mode"), lax.axis_index("col")
    cols = lax.axis_size("col")
    right, left = (col + 1) % cols, (col + cols - 1) % cols
    partners = [((me // 2 + dy) % 4) * 2 + (me % 2 + dx) % 2 for dy, dx in PARTNERS]

    barrier = pltpu.get_barrier_semaphore()
    for part in partners:
        pl.semaphore_signal(barrier, inc=1, device_id=(part, col), device_id_type=MESH)
    for side in (right, left):
        pl.semaphore_signal(barrier, inc=1, device_id=(me, side), device_id_type=MESH)

    planes = fv.reshape(2, 2 * LOCAL, ROWS, 128)

    def load(chunk, half):
        rows = pl.ds(16 * chunk, 16)
        return pltpu.make_async_copy(
            fields.at[:, rows, pl.ds(128 * half, 128)], planes.at[half, :, rows, :], in_sem.at[chunk, half]
        )

    for chunk in range(CHUNKS):
        for half in range(2):
            load(chunk, half).start()
    tables = [
        pltpu.make_async_copy(evaluate, ev, table_sem.at[0]),
        pltpu.make_async_copy(project, pj, table_sem.at[1]),
    ]
    for table in tables:
        table.start()

    def prepare(chunk):
        def one(dest, carry):
            row = 16 * chunk + 2 * dest
            values = []
            for j in range(2):
                values.append([])
                for g in range(TILES):
                    rows = pl.ds(8 * g * ROWS + row + j, 8, stride=ROWS)
                    values[j].append(jnp.concatenate([fv[0, rows, :], fv[1, rows, :]], axis=1))
                for g in range(TILES):
                    ft[g, row + j + 1, :, :COLS] = values[j][g]
            for j in range(2):
                for k, g in enumerate((0, 2, 5, 7)):
                    pair = jnp.concatenate([values[j][g], values[j][g + 1]], axis=0)
                    snd[dest, chunk, 64 * j + 16 * k : 64 * j + 16 * k + 16, :] = pair.astype(BF16)
            pair = jnp.concatenate([values[0][4], values[1][4]], axis=0)
            snd[dest, chunk, 128:144, :] = pair.astype(BF16)
            return carry

        lax.fori_loop(0, PARTS, one, 0)

    def forward(chunk, k):
        part = partners[k]
        return pltpu.make_async_remote_copy(
            src_ref=snd.at[part, chunk], dst_ref=rcv.at[chunk, me],
            send_sem=fs_sem.at[chunk, k], recv_sem=fr_sem.at[chunk, me],
            device_id=(part, col), device_id_type=MESH,
        )

    def forward_in(chunk, k):
        part = partners[k]
        return pltpu.make_async_remote_copy(
            src_ref=snd.at[part, chunk], dst_ref=rcv.at[chunk, part],
            send_sem=fs_sem.at[chunk, k], recv_sem=fr_sem.at[chunk, part],
            device_id=(part, col), device_id_type=MESH,
        )

    def own(chunk):
        return pltpu.make_async_copy(snd.at[me, chunk], rcv.at[chunk, me], own_sem.at[chunk])

    for half in range(2):
        load(0, half).wait()
    prepare(0)
    pl.semaphore_wait(barrier, len(PARTNERS) + 2)
    for chunk in range(CHUNKS):
        if chunk > 0:
            for half in range(2):
                load(chunk, half).wait()
            prepare(chunk)
        for k in range(len(PARTNERS)):
            forward(chunk, k).start()
        own(chunk).start()

    for g in range(TILES):
        ft[g, 0, :, :] = jnp.zeros((8, COLS), F32)
        ft[g, ROWS + 1, :, :] = jnp.zeros((8, COLS), F32)
    for ref in (ita, itb):
        ref[0, :, :] = jnp.zeros((8, COLS), F32)
        ref[ROWS + 1, :, :] = jnp.zeros((8, COLS), F32)
    for table in tables:
        table.wait()
    mode = iota((MODES, DEPTH), 0)
    slot = iota((MODES, DEPTH), 1)
    mixed = slot - 256
    for f in range(2):
        main_mode = LOCAL * (slot >> 5) + (slot & 31) + 4 * f
        place = mixed & 7
        mix_mode = LOCAL * (mixed >> 4) + (place - 4 if f else place + 32)
        for j in range(2):
            mine = (((mixed >> 3) & 1) == j) & ((place >= 4) if f else (place < 4))
            want = jnp.where(slot < 256, main_mode, jnp.where(mine, mix_mode, -1))
            onehot = jnp.where(want == mode, 1.0, 0.0).astype(BF16)
            weights[2 * f + j] = lax.dot_general(
                ev[...], onehot, (((0,), (0,)), ((), ())), preferred_element_type=F32
            ).astype(BF16)
    mode = iota((OUT_ROWS, MODES), 1)
    slot = iota((OUT_ROWS, MODES), 0)
    mixed = slot - 256
    for f in range(2):
        main_mode = LOCAL * (slot >> 5) + (slot & 31) + 4 * f
        place = mixed & 7
        mix_mode = LOCAL * (mixed >> 3) + (place - 4 if f else place + 32)
        mine = (place >= 4) if f else (place < 4)
        want = jnp.where(slot < 256, main_mode, jnp.where(mine, mix_mode, -1))
        onehot = jnp.where(want == mode, 1.0, 0.0).astype(BF16)
        proj[f, :, 1536:] = jnp.zeros((OUT_ROWS, 128), BF16)
        proj[f, :, :POINTS] = jnp.dot(onehot, pj[...], preferred_element_type=F32).astype(BF16)
        reacted[f, POINTS:, :] = jnp.zeros((PADDED - POINTS, 2 * COLS), BF16)
    eye = iota((128, 128), 0) == iota((128, 128), 1)
    for q in (*range(0, POINTS - 128, 128), POINTS - 128):
        supply = feed[q : q + 128].reshape(1, 128)
        for f, rate in enumerate((supply, supply + kill[q : q + 128].reshape(1, 128))):
            column = jnp.sum(jnp.where(eye, jnp.broadcast_to(rate, (128, 128)), 0.0), axis=1, keepdims=True)
            rate_b[f, q : q + 128, :] = jnp.broadcast_to(column, (128, 128))

    def arrive(chunk):
        for k in range(len(PARTNERS)):
            forward_in(chunk, k).wait_recv()
        own(chunk).wait()

    def react(chunk):
        def block(b, carry):
            rows = pl.ds(pl.multiple_of(b * BLOCK, 16), BLOCK)
            feed = jnp.tile(rate_b[0, rows, :], (1, 2))
            loss = jnp.tile(rate_b[1, rows, :], (1, 2))
            for j in range(2):
                mix = rcv[chunk, :, 128:144, :].reshape(128, COLS)
                ub = jnp.concatenate([rcv[chunk, :, 64 * j : 64 * j + 32, :].reshape(256, COLS), mix], axis=0)
                vb = jnp.concatenate([rcv[chunk, :, 64 * j + 32 : 64 * j + 64, :].reshape(256, COLS), mix], axis=0)
                u = jnp.dot(weights[j, rows, :], ub, preferred_element_type=F32)
                v = jnp.dot(weights[2 + j, rows, :], vb, preferred_element_type=F32)
                squared = u * v * v
                lanes = slice(COLS * j, COLS * j + COLS)
                reacted[0, rows, lanes] = (feed * (1.0 - u) - squared).astype(BF16)
                reacted[1, rows, lanes] = (squared - loss * v).astype(BF16)
            return carry

        lax.fori_loop(0, POINTS // BLOCK, block, 0)

    def project_back(chunk):
        mix = None
        for f in range(2):
            total = jnp.dot(proj[f], reacted[f], preferred_element_type=F32)
            main = jnp.stack(
                [total[:256, :COLS].reshape(32, 8, COLS), total[:256, COLS:].reshape(32, 8, COLS)], axis=1
            ).astype(BF16)
            bsnd[:, 5 * f : 5 * f + 4, chunk] = main.reshape(PARTS, 4, 16, COLS)
            mix = total[256:] if f == 0 else mix + total[256:]
        mix = jnp.stack([mix[:, :COLS].reshape(8, 8, COLS), mix[:, COLS:].reshape(8, 8, COLS)], axis=1)
        bsnd[:, 4, chunk] = mix.astype(BF16).reshape(PARTS, 16, COLS)

    def backward(g, k, low=0, high=CHUNKS, incoming=False):
        part = partners[k]
        slot = part if incoming else me
        return pltpu.make_async_remote_copy(
            src_ref=bsnd.at[part, g, low:high], dst_ref=brcv.at[slot, g, low:high],
            send_sem=bs_sem.at[g, k], recv_sem=br_sem.at[g, slot],
            device_id=(part, col), device_id_type=MESH,
        )

    def back_own(g, low=0, high=CHUNKS):
        return pltpu.make_async_copy(bsnd.at[me, g, low:high], brcv.at[me, g, low:high], bown_sem.at[g])

    def send_back(g, low=0, high=CHUNKS):
        for k in range(len(PARTNERS)):
            backward(g, k, low, high).start()
        back_own(g, low, high).start()

    def work(chunk):
        react(chunk)
        project_back(chunk)

    def early(chunk, carry):
        arrive(chunk)
        work(chunk)
        return carry

    lax.fori_loop(0, CHUNKS - 1, early, 0)
    arrive(CHUNKS - 1)
    for g in range(EARLY):
        send_back(g, 0, CHUNKS - 1)
    work(CHUNKS - 1)
    for g in range(EARLY):
        send_back(g, CHUNKS - 1, CHUNKS)
    for g in range(EARLY, WINDOW):
        send_back(g)

    lane = iota((8, 128), 1)

    def gather(g):
        for k in range(len(PARTNERS)):
            backward(g, k, incoming=True).wait_recv()
        back_own(g).wait()

        def rows16(c, carry):
            packed = jnp.zeros((8, 128), F32)
            for s in range(PARTS):
                pair = brcv[s, g, c].astype(F32)
                for j in range(2):
                    row = 16 * c + 2 * s + j + 1
                    value = ft[g, row, :, :COLS] + TIME_STEP * pair[8 * j : 8 * j + 8]
                    ft[g, row, :, :COLS] = value
                    edge = jnp.where(lane < 64, value[:, :128], value[:, 128:])
                    at = 2 * s + j
                    packed = jnp.where((lane >> 3) == at, pltpu.roll(edge, (8 * at + 4) % 128, 1), packed)
            hsnd[g, c] = packed
            return carry

        lax.fori_loop(0, CHUNKS, rows16, 0)

    def halo(g, side, incoming=False):
        there = 1 - side if incoming else side
        return pltpu.make_async_remote_copy(
            src_ref=hsnd.at[g], dst_ref=hrcv.at[there, g],
            send_sem=hs_sem.at[g, side], recv_sem=hr_sem.at[g, there],
            device_id=(me, left if side else right), device_id_type=MESH,
        )

    def sweeps(g):
        for side in range(2):
            halo(g, side, True).wait_recv()
        pair = 8 * g + iota((8, 128), 0)
        weight = jnp.where(pair < LOCAL, DIFFUSION[0], DIFFUSION[1])
        keep = 1.0 / (1.0 + 4.0 * weight)
        near = weight / (1.0 + 4.0 * weight)

        low = (lane & 7) < 4
        lefts = [jnp.where(low, hrcv[0, g, c], hsnd[g, c]) for c in range(CHUNKS)]
        rights = [jnp.where(low, hsnd[g, c], hrcv[1, g, c]) for c in range(CHUNKS)]
        left_base, right_base = lefts, rights

        def seam(now, base):
            later = []
            downs = [pltpu.roll(x, 8, 1) for x in now]
            ups = [pltpu.roll(x, 120, 1) for x in now]
            for c in range(CHUNKS):
                total = jnp.where(lane < 8, downs[c - 1] if c else 0.0, downs[c])
                total = total + jnp.where(lane >= 120, ups[c + 1] if c + 1 < CHUNKS else 0.0, ups[c])
                total = total + (pltpu.roll(now[c], 1, 1) + pltpu.roll(now[c], 127, 1))
                later.append(keep * base[c] + near * total)
            return later

        def row(ref, r):
            return [ref[r, :, :128], ref[r, :, 128:]]

        start = ft.at[g]

        def sweep(source, store):
            beside = [
                jnp.where((lane & 7) == 3, x, pltpu.roll(y, 126, 1)) for x, y in zip(lefts, rights, strict=True)
            ]
            up, middle = row(source, 0), row(source, 1)
            for r in range(1, ROWS + 1):
                down = row(source, r + 1)
                base = row(start, r) if source is not start else middle
                after = [pltpu.roll(t, 1, 1) for t in middle]
                before = [pltpu.roll(t, 127, 1) for t in middle]
                edge = pltpu.roll(beside[(r - 1) // 16], (125 - 8 * ((r - 1) % 16)) % 128, 1)
                sides = [
                    jnp.where(lane == 0, edge, after[0]) + jnp.where(lane == 127, before[1], before[0]),
                    jnp.where(lane == 0, after[0], after[1]) + jnp.where(lane == 127, edge, before[1]),
                ]
                store(r, [keep * base[t] + near * ((up[t] + down[t]) + sides[t]) for t in range(2)])
                up, middle = middle, down

        def into(ref):
            def store(r, result):
                ref[r, :, :128] = result[0]
                ref[r, :, 128:] = result[1]

            return store

        def last_store(r, result):
            rows = pl.ds(8 * g * ROWS + r - 1, 8, stride=ROWS)
            fv[0, rows, :] = result[0]
            fv[1, rows, :] = result[1]

        source = start
        for store_ref in (ita, itb, ita):
            sweep(source, into(store_ref))
            source = store_ref
            lefts, rights = seam(lefts, left_base), seam(rights, right_base)
        sweep(source, last_store)

    def write(g, half):
        rows = pl.ds(8 * g, 8)
        return pltpu.make_async_copy(
            planes.at[half, rows], out.at[rows, :, pl.ds(128 * half, 128)], out_sem.at[g, half]
        )

    def turn(i, carry):
        @pl.when(i < TILES)
        def _():
            gather(i)
            for side in range(2):
                halo(i, side).start()

        @pl.when(i + WINDOW < TILES)
        def _():
            send_back(i + WINDOW)

        @pl.when(i >= LAG)
        def _():
            sweeps(i - LAG)
            for half in range(2):
                write(i - LAG, half).start()

        return carry

    lax.fori_loop(0, TILES + LAG, turn, 0)

    for chunk in range(CHUNKS):
        for k in range(len(PARTNERS)):
            forward(chunk, k).wait_send()

    def finish(g, carry):
        for k in range(len(PARTNERS)):
            backward(g, k).wait_send()
        for side in range(2):
            halo(g, side).wait_send()
            write(g, side).wait()
        return carry

    lax.fori_loop(0, TILES, finish, 0)


def hand_over(source, target, held, in_sem, out_sem):
    rows = [pl.ds(8 * g, 8) for g in range(TILES)]
    reads = [pltpu.make_async_copy(source.at[r], held.at[r], in_sem.at[g]) for g, r in enumerate(rows)]
    writes = [pltpu.make_async_copy(held.at[r], target.at[r], out_sem.at[g]) for g, r in enumerate(rows)]
    for read in reads:
        read.start()
    for read, write in zip(reads, writes, strict=True):
        read.wait()
        write.start()
    for write in writes:
        write.wait()


def body(fields, evaluate, project, feed, kill):
    partners = len(PARTNERS)
    hbm = pl.BlockSpec(memory_space=pltpu.MemorySpace.HBM)
    vmem = pl.BlockSpec(memory_space=pltpu.VMEM)
    dma = pltpu.SemaphoreType.DMA
    stepped = pl.pallas_call(
        kernel,
        out_shape=jax.ShapeDtypeStruct((2 * LOCAL, ROWS, COLS), F32),
        in_specs=[hbm, hbm, hbm, vmem, vmem],
        out_specs=pl.BlockSpec(memory_space=pl.ANY),
        scratch_shapes=[
            pltpu.VMEM((2, 2 * LOCAL * ROWS, 128), F32),
            pltpu.VMEM((TILES, ROWS + 2, 8, COLS), F32),
            pltpu.VMEM((ROWS + 2, 8, COLS), F32),
            pltpu.VMEM((ROWS + 2, 8, COLS), F32),
            pltpu.VMEM((MODES, POINTS), BF16),
            pltpu.VMEM((MODES, POINTS), BF16),
            pltpu.VMEM((4, POINTS, DEPTH), BF16),
            pltpu.VMEM((2, OUT_ROWS, PADDED), BF16),
            pltpu.VMEM((2, POINTS, 128), F32),
            pltpu.VMEM((PARTS, CHUNKS, MESSAGE, COLS), BF16),
            pltpu.VMEM((CHUNKS, PARTS, MESSAGE, COLS), BF16),
            pltpu.VMEM((2, PADDED, 2 * COLS), BF16),
            pltpu.VMEM((PARTS, TILES, CHUNKS, 16, COLS), BF16),
            pltpu.VMEM((PARTS, TILES, CHUNKS, 16, COLS), BF16),
            pltpu.VMEM((TILES, CHUNKS, 8, 128), F32),
            pltpu.VMEM((2, TILES, CHUNKS, 8, 128), F32),
            dma((CHUNKS, 2)),
            dma((2,)),
            dma((TILES, 2)),
            dma((CHUNKS,)),
            dma((CHUNKS, partners)),
            dma((CHUNKS, PARTS)),
            dma((TILES,)),
            dma((TILES, partners)),
            dma((TILES, PARTS)),
            dma((TILES, 2)),
            dma((TILES, 2)),
        ],
        compiler_params=pltpu.CompilerParams(
            collective_id=0, has_side_effects=True, vmem_limit_bytes=VMEM_LIMIT
        ),
        cost_estimate=pl.CostEstimate(
            flops=8 * 2 * LOCAL * ROWS * COLS * POINTS // 2, bytes_accessed=12 * 2**20, transcendentals=0
        ),
    )(fields.reshape(2 * LOCAL, ROWS, COLS), evaluate.T, project, feed, kill)
    stepped = pl.pallas_call(
        hand_over,
        out_shape=jax.ShapeDtypeStruct((2 * LOCAL, ROWS, COLS), F32),
        in_specs=[hbm],
        out_specs=hbm,
        scratch_shapes=[pltpu.VMEM((2 * LOCAL, ROWS, COLS), F32), dma((TILES,)), dma((TILES,))],
        compiler_params=pltpu.CompilerParams(vmem_limit_bytes=VMEM_LIMIT),
    )(stepped)
    return stepped.reshape(2, LOCAL, ROWS, COLS)


def solution(mesh):
    in_specs = (P(None, "mode", None, "col"), P(), P(), P(), P())
    out_specs = P(None, "mode", None, "col")
    return jax.shard_map(body, mesh=mesh, in_specs=in_specs, out_specs=out_specs, check_vma=False)
```

```python
import jax
import jax.numpy as jnp
from jax import lax
from jax.experimental import pallas as pl
from jax.experimental.pallas import tpu as pltpu
from jax.sharding import PartitionSpec as P

MESH = pl.DeviceIdType.MESH
F32, BF16 = jnp.float32, jnp.bfloat16

VMEM_LIMIT = 58 * 2**20
TIME_STEP = 0.5
DIFFUSION = (1.0, 0.5)

MODES, POINTS = 288, 1584
PARTS = 8
LOCAL = 36
ROWS, COLS = 64, 256
CHUNKS = 4
TILES = 9
MESSAGE = 144
DEPTH = 384
PADDED = 1664
BLOCK = 528
OUT_ROWS = 320
WINDOW = 3
LAG = 2
LATE = 1
SWEPT = TILES - LATE
EARLY = 2
PARTNERS = ((0, 1), (1, 0), (3, 0), (2, 0), (1, 1), (3, 1), (2, 1))


def iota(shape, dim):
    return lax.broadcasted_iota(jnp.int32, shape, dim)


def sweep_tile(g, start, own_edge, left_edge, right_edge, ita, itb, fv, place):
    lane = iota((8, 128), 1)
    pair = 8 * g + iota((8, 128), 0)
    weight = jnp.where(pair < LOCAL, DIFFUSION[0], DIFFUSION[1])
    keep = 1.0 / (1.0 + 4.0 * weight)
    near = weight / (1.0 + 4.0 * weight)

    low = (lane & 7) < 4
    lefts = [jnp.where(low, left_edge[c], own_edge[c]) for c in range(CHUNKS)]
    rights = [jnp.where(low, own_edge[c], right_edge[c]) for c in range(CHUNKS)]
    left_base, right_base = lefts, rights

    def seam(now, base):
        later = []
        downs = [pltpu.roll(x, 8, 1) for x in now]
        ups = [pltpu.roll(x, 120, 1) for x in now]
        for c in range(CHUNKS):
            total = jnp.where(lane < 8, downs[c - 1] if c else 0.0, downs[c])
            total = total + jnp.where(lane >= 120, ups[c + 1] if c + 1 < CHUNKS else 0.0, ups[c])
            total = total + (pltpu.roll(now[c], 1, 1) + pltpu.roll(now[c], 127, 1))
            later.append(keep * base[c] + near * total)
        return later

    def row(ref, r):
        return [ref[r, :, :128], ref[r, :, 128:]]

    def sweep(source, store):
        beside = [
            jnp.where((lane & 7) == 3, x, pltpu.roll(y, 126, 1)) for x, y in zip(lefts, rights, strict=True)
        ]
        up, middle = row(source, 0), row(source, 1)
        for r in range(1, ROWS + 1):
            down = row(source, r + 1)
            base = row(start, r) if source is not start else middle
            after = [pltpu.roll(t, 1, 1) for t in middle]
            before = [pltpu.roll(t, 127, 1) for t in middle]
            edge = pltpu.roll(beside[(r - 1) // 16], (125 - 8 * ((r - 1) % 16)) % 128, 1)
            sides = [
                jnp.where(lane == 0, edge, after[0]) + jnp.where(lane == 127, before[1], before[0]),
                jnp.where(lane == 0, after[0], after[1]) + jnp.where(lane == 127, edge, before[1]),
            ]
            store(r, [keep * base[t] + near * ((up[t] + down[t]) + sides[t]) for t in range(2)])
            up, middle = middle, down

    def into(ref):
        def store(r, result):
            ref[r, :, :128] = result[0]
            ref[r, :, 128:] = result[1]

        return store

    def last_store(r, result):
        rows = pl.ds(8 * place * ROWS + r - 1, 8, stride=ROWS)
        fv[0, rows, :] = result[0]
        fv[1, rows, :] = result[1]

    source = start
    for store_ref in (ita, itb, ita):
        sweep(source, into(store_ref))
        source = store_ref
        lefts, rights = seam(lefts, left_base), seam(rights, right_base)
    sweep(source, last_store)


def kernel(
    fields, evaluate, project, feed, kill, out, rs_out, edge_out,
    fv, ft, ita, itb, ev, pj, weights, proj, rate_b,
    snd, rcv, reacted, bsnd, brcv, hsnd, hrcv,
    in_sem, table_sem, out_sem, own_sem, fs_sem, fr_sem, bown_sem, bs_sem, br_sem, hs_sem, hr_sem, late_sem,
):
    me, col = lax.axis_index("mode"), lax.axis_index("col")
    cols = lax.axis_size("col")
    right, left = (col + 1) % cols, (col + cols - 1) % cols
    partners = [((me // 2 + dy) % 4) * 2 + (me % 2 + dx) % 2 for dy, dx in PARTNERS]

    barrier = pltpu.get_barrier_semaphore()
    for part in partners:
        pl.semaphore_signal(barrier, inc=1, device_id=(part, col), device_id_type=MESH)
    for side in (right, left):
        pl.semaphore_signal(barrier, inc=1, device_id=(me, side), device_id_type=MESH)

    planes = fv.reshape(2, 2 * LOCAL, ROWS, 128)

    def load(chunk, half):
        rows = pl.ds(16 * chunk, 16)
        return pltpu.make_async_copy(
            fields.at[:, rows, pl.ds(128 * half, 128)], planes.at[half, :, rows, :], in_sem.at[chunk, half]
        )

    for chunk in range(CHUNKS):
        for half in range(2):
            load(chunk, half).start()
    tables = [
        pltpu.make_async_copy(evaluate, ev, table_sem.at[0]),
        pltpu.make_async_copy(project, pj, table_sem.at[1]),
    ]
    for table in tables:
        table.start()

    def prepare(chunk):
        def one(dest, carry):
            row = 16 * chunk + 2 * dest
            values = []
            for j in range(2):
                values.append([])
                for g in range(TILES):
                    rows = pl.ds(8 * g * ROWS + row + j, 8, stride=ROWS)
                    values[j].append(jnp.concatenate([fv[0, rows, :], fv[1, rows, :]], axis=1))
                for g in range(TILES):
                    ft[g, row + j + 1, :, :COLS] = values[j][g]
            for j in range(2):
                for k, g in enumerate((0, 2, 5, 7)):
                    pair = jnp.concatenate([values[j][g], values[j][g + 1]], axis=0)
                    snd[dest, chunk, 64 * j + 16 * k : 64 * j + 16 * k + 16, :] = pair.astype(BF16)
            pair = jnp.concatenate([values[0][4], values[1][4]], axis=0)
            snd[dest, chunk, 128:144, :] = pair.astype(BF16)
            return carry

        lax.fori_loop(0, PARTS, one, 0)

    def forward(chunk, k):
        part = partners[k]
        return pltpu.make_async_remote_copy(
            src_ref=snd.at[part, chunk], dst_ref=rcv.at[chunk, me],
            send_sem=fs_sem.at[chunk, k], recv_sem=fr_sem.at[chunk, me],
            device_id=(part, col), device_id_type=MESH,
        )

    def forward_in(chunk, k):
        part = partners[k]
        return pltpu.make_async_remote_copy(
            src_ref=snd.at[part, chunk], dst_ref=rcv.at[chunk, part],
            send_sem=fs_sem.at[chunk, k], recv_sem=fr_sem.at[chunk, part],
            device_id=(part, col), device_id_type=MESH,
        )

    def own(chunk):
        return pltpu.make_async_copy(snd.at[me, chunk], rcv.at[chunk, me], own_sem.at[chunk])

    for half in range(2):
        load(0, half).wait()
    prepare(0)
    pl.semaphore_wait(barrier, len(PARTNERS) + 2)
    for chunk in range(CHUNKS):
        if chunk > 0:
            for half in range(2):
                load(chunk, half).wait()
            prepare(chunk)
        for k in range(len(PARTNERS)):
            forward(chunk, k).start()
        own(chunk).start()

    for g in range(TILES):
        ft[g, 0, :, :] = jnp.zeros((8, COLS), F32)
        ft[g, ROWS + 1, :, :] = jnp.zeros((8, COLS), F32)
    for ref in (ita, itb):
        ref[0, :, :] = jnp.zeros((8, COLS), F32)
        ref[ROWS + 1, :, :] = jnp.zeros((8, COLS), F32)
    for table in tables:
        table.wait()
    mode = iota((MODES, DEPTH), 0)
    slot = iota((MODES, DEPTH), 1)
    mixed = slot - 256
    for f in range(2):
        main_mode = LOCAL * (slot >> 5) + (slot & 31) + 4 * f
        place = mixed & 7
        mix_mode = LOCAL * (mixed >> 4) + (place - 4 if f else place + 32)
        for j in range(2):
            mine = (((mixed >> 3) & 1) == j) & ((place >= 4) if f else (place < 4))
            want = jnp.where(slot < 256, main_mode, jnp.where(mine, mix_mode, -1))
            onehot = jnp.where(want == mode, 1.0, 0.0).astype(BF16)
            weights[2 * f + j] = lax.dot_general(
                ev[...], onehot, (((0,), (0,)), ((), ())), preferred_element_type=F32
            ).astype(BF16)
    mode = iota((OUT_ROWS, MODES), 1)
    slot = iota((OUT_ROWS, MODES), 0)
    mixed = slot - 256
    for f in range(2):
        main_mode = LOCAL * (slot >> 5) + (slot & 31) + 4 * f
        place = mixed & 7
        mix_mode = LOCAL * (mixed >> 3) + (place - 4 if f else place + 32)
        mine = (place >= 4) if f else (place < 4)
        want = jnp.where(slot < 256, main_mode, jnp.where(mine, mix_mode, -1))
        onehot = jnp.where(want == mode, 1.0, 0.0).astype(BF16)
        proj[f, :, 1536:] = jnp.zeros((OUT_ROWS, 128), BF16)
        proj[f, :, :POINTS] = jnp.dot(onehot, pj[...], preferred_element_type=F32).astype(BF16)
        reacted[f, POINTS:, :] = jnp.zeros((PADDED - POINTS, 2 * COLS), BF16)
    eye = iota((128, 128), 0) == iota((128, 128), 1)
    for q in (*range(0, POINTS - 128, 128), POINTS - 128):
        supply = feed[q : q + 128].reshape(1, 128)
        for f, rate in enumerate((supply, supply + kill[q : q + 128].reshape(1, 128))):
            column = jnp.sum(jnp.where(eye, jnp.broadcast_to(rate, (128, 128)), 0.0), axis=1, keepdims=True)
            rate_b[f, q : q + 128, :] = jnp.broadcast_to(column, (128, 128))

    def arrive(chunk):
        for k in range(len(PARTNERS)):
            forward_in(chunk, k).wait_recv()
        own(chunk).wait()

    def react(chunk):
        def block(b, carry):
            rows = pl.ds(pl.multiple_of(b * BLOCK, 16), BLOCK)
            feed = jnp.tile(rate_b[0, rows, :], (1, 2))
            loss = jnp.tile(rate_b[1, rows, :], (1, 2))
            for j in range(2):
                mix = rcv[chunk, :, 128:144, :].reshape(128, COLS)
                ub = jnp.concatenate([rcv[chunk, :, 64 * j : 64 * j + 32, :].reshape(256, COLS), mix], axis=0)
                vb = jnp.concatenate([rcv[chunk, :, 64 * j + 32 : 64 * j + 64, :].reshape(256, COLS), mix], axis=0)
                u = jnp.dot(weights[j, rows, :], ub, preferred_element_type=F32)
                v = jnp.dot(weights[2 + j, rows, :], vb, preferred_element_type=F32)
                squared = u * v * v
                lanes = slice(COLS * j, COLS * j + COLS)
                reacted[0, rows, lanes] = (feed * (1.0 - u) - squared).astype(BF16)
                reacted[1, rows, lanes] = (squared - loss * v).astype(BF16)
            return carry

        lax.fori_loop(0, POINTS // BLOCK, block, 0)

    def project_back(chunk):
        mix = None
        for f in range(2):
            total = jnp.dot(proj[f], reacted[f], preferred_element_type=F32)
            main = jnp.stack(
                [total[:256, :COLS].reshape(32, 8, COLS), total[:256, COLS:].reshape(32, 8, COLS)], axis=1
            ).astype(BF16)
            bsnd[:, 5 * f : 5 * f + 4, chunk] = main.reshape(PARTS, 4, 16, COLS)
            mix = total[256:] if f == 0 else mix + total[256:]
        mix = jnp.stack([mix[:, :COLS].reshape(8, 8, COLS), mix[:, COLS:].reshape(8, 8, COLS)], axis=1)
        bsnd[:, 4, chunk] = mix.astype(BF16).reshape(PARTS, 16, COLS)

    def backward(g, k, low=0, high=CHUNKS, incoming=False):
        part = partners[k]
        slot = part if incoming else me
        return pltpu.make_async_remote_copy(
            src_ref=bsnd.at[part, g, low:high], dst_ref=brcv.at[slot, g, low:high],
            send_sem=bs_sem.at[g, k], recv_sem=br_sem.at[g, slot],
            device_id=(part, col), device_id_type=MESH,
        )

    def back_own(g, low=0, high=CHUNKS):
        return pltpu.make_async_copy(bsnd.at[me, g, low:high], brcv.at[me, g, low:high], bown_sem.at[g])

    def send_back(g, low=0, high=CHUNKS):
        for k in range(len(PARTNERS)):
            backward(g, k, low, high).start()
        back_own(g, low, high).start()

    def work(chunk):
        react(chunk)
        project_back(chunk)

    def early(chunk, carry):
        arrive(chunk)
        work(chunk)
        return carry

    lax.fori_loop(0, CHUNKS - 1, early, 0)
    arrive(CHUNKS - 1)
    for g in range(EARLY):
        send_back(g, 0, CHUNKS - 1)
    work(CHUNKS - 1)
    for g in range(EARLY):
        send_back(g, CHUNKS - 1, CHUNKS)
    for g in range(EARLY, WINDOW):
        send_back(g)

    lane = iota((8, 128), 1)

    def gather(g):
        for k in range(len(PARTNERS)):
            backward(g, k, incoming=True).wait_recv()
        back_own(g).wait()

        def rows16(c, carry):
            packed = jnp.zeros((8, 128), F32)
            for s in range(PARTS):
                pair = brcv[s, g, c].astype(F32)
                for j in range(2):
                    row = 16 * c + 2 * s + j + 1
                    value = ft[g, row, :, :COLS] + TIME_STEP * pair[8 * j : 8 * j + 8]
                    ft[g, row, :, :COLS] = value
                    edge = jnp.where(lane < 64, value[:, :128], value[:, 128:])
                    at = 2 * s + j
                    packed = jnp.where((lane >> 3) == at, pltpu.roll(edge, (8 * at + 4) % 128, 1), packed)
            hsnd[g, c] = packed
            return carry

        lax.fori_loop(0, CHUNKS, rows16, 0)

    def halo(g, side, incoming=False):
        there = 1 - side if incoming else side
        return pltpu.make_async_remote_copy(
            src_ref=hsnd.at[g], dst_ref=hrcv.at[there, g],
            send_sem=hs_sem.at[g, side], recv_sem=hr_sem.at[g, there],
            device_id=(me, left if side else right), device_id_type=MESH,
        )

    def sweeps(g):
        for side in range(2):
            halo(g, side, True).wait_recv()
        own_edge, left_edge, right_edge = [
            [part[c] for c in range(CHUNKS)] for part in (hsnd.at[g], hrcv.at[0, g], hrcv.at[1, g])
        ]
        sweep_tile(g, ft.at[g], own_edge, left_edge, right_edge, ita, itb, fv, g)

    def write(g, half):
        rows = pl.ds(8 * g, 8)
        return pltpu.make_async_copy(
            planes.at[half, rows], out.at[rows, :, pl.ds(128 * half, 128)], out_sem.at[g, half]
        )

    def turn(i, carry):
        @pl.when(i < TILES)
        def _():
            gather(i)
            for side in range(2):
                halo(i, side).start()

        @pl.when(i + WINDOW < TILES)
        def _():
            send_back(i + WINDOW)

        @pl.when(i >= LAG)
        def _():
            sweeps(i - LAG)
            for half in range(2):
                write(i - LAG, half).start()

        return carry

    lax.fori_loop(0, TILES + LAG - LATE, turn, 0)

    late = [pltpu.make_async_copy(ft.at[SWEPT:], rs_out, late_sem.at[0])]
    late.append(pltpu.make_async_copy(hsnd.at[SWEPT:], edge_out.at[0], late_sem.at[1]))
    for side in range(2):
        late.append(pltpu.make_async_copy(hrcv.at[side, SWEPT:], edge_out.at[1 + side], late_sem.at[2 + side]))
    for copy in late[:2]:
        copy.start()
    for g in range(SWEPT, TILES):
        for side in range(2):
            halo(g, side, True).wait_recv()
    for copy in late[2:]:
        copy.start()

    for chunk in range(CHUNKS):
        for k in range(len(PARTNERS)):
            forward(chunk, k).wait_send()

    def finish(g, carry):
        for k in range(len(PARTNERS)):
            backward(g, k).wait_send()
        for side in range(2):
            halo(g, side).wait_send()

        @pl.when(g < SWEPT)
        def _():
            for half in range(2):
                write(g, half).wait()

        return carry

    lax.fori_loop(0, TILES, finish, 0)
    for copy in late:
        copy.wait()


def hand_over(source, rs, edges, target, held, ft, near, ita, itb, fv, in_sem, late_sem, out_sem, done_sem):
    first = [pltpu.make_async_copy(rs, ft, late_sem.at[0]), pltpu.make_async_copy(edges, near, late_sem.at[1])]
    rows = [pl.ds(8 * g, 8) for g in range(TILES)]
    reads = [pltpu.make_async_copy(source.at[rows[g]], held.at[rows[g]], in_sem.at[g]) for g in range(SWEPT)]
    writes = [pltpu.make_async_copy(held.at[rows[g]], target.at[rows[g]], out_sem.at[g]) for g in range(SWEPT)]
    for copy in first + reads:
        copy.start()
    for ref in (ita, itb):
        ref[0, :, :] = jnp.zeros((8, COLS), F32)
        ref[ROWS + 1, :, :] = jnp.zeros((8, COLS), F32)
    for copy in first:
        copy.wait()
    for read, write in zip(reads, writes, strict=True):
        read.wait()
        write.start()
    planes = fv.reshape(2, 8 * LATE, ROWS, 128)
    last = []
    for i in range(LATE):
        own_edge, left_edge, right_edge = [[near[k, i, c] for c in range(CHUNKS)] for k in range(3)]
        sweep_tile(SWEPT + i, ft.at[i], own_edge, left_edge, right_edge, ita, itb, fv, i)
        for half in range(2):
            lanes = pl.ds(128 * half, 128)
            copy = pltpu.make_async_copy(
                planes.at[half, pl.ds(8 * i, 8)], target.at[rows[SWEPT + i], :, lanes], done_sem.at[i, half]
            )
            copy.start()
            last.append(copy)
    for copy in writes + last:
        copy.wait()


def body(fields, evaluate, project, feed, kill):
    partners = len(PARTNERS)
    hbm = pl.BlockSpec(memory_space=pltpu.MemorySpace.HBM)
    vmem = pl.BlockSpec(memory_space=pltpu.VMEM)
    dma = pltpu.SemaphoreType.DMA
    stepped, rs, edges = pl.pallas_call(
        kernel,
        out_shape=[
            jax.ShapeDtypeStruct((2 * LOCAL, ROWS, COLS), F32),
            jax.ShapeDtypeStruct((LATE, ROWS + 2, 8, COLS), F32),
            jax.ShapeDtypeStruct((3, LATE, CHUNKS, 8, 128), F32),
        ],
        in_specs=[hbm, hbm, hbm, vmem, vmem],
        out_specs=[hbm] * 3,
        scratch_shapes=[
            pltpu.VMEM((2, 2 * LOCAL * ROWS, 128), F32),
            pltpu.VMEM((TILES, ROWS + 2, 8, COLS), F32),
            pltpu.VMEM((ROWS + 2, 8, COLS), F32),
            pltpu.VMEM((ROWS + 2, 8, COLS), F32),
            pltpu.VMEM((MODES, POINTS), BF16),
            pltpu.VMEM((MODES, POINTS), BF16),
            pltpu.VMEM((4, POINTS, DEPTH), BF16),
            pltpu.VMEM((2, OUT_ROWS, PADDED), BF16),
            pltpu.VMEM((2, POINTS, 128), F32),
            pltpu.VMEM((PARTS, CHUNKS, MESSAGE, COLS), BF16),
            pltpu.VMEM((CHUNKS, PARTS, MESSAGE, COLS), BF16),
            pltpu.VMEM((2, PADDED, 2 * COLS), BF16),
            pltpu.VMEM((PARTS, TILES, CHUNKS, 16, COLS), BF16),
            pltpu.VMEM((PARTS, TILES, CHUNKS, 16, COLS), BF16),
            pltpu.VMEM((TILES, CHUNKS, 8, 128), F32),
            pltpu.VMEM((2, TILES, CHUNKS, 8, 128), F32),
            dma((CHUNKS, 2)),
            dma((2,)),
            dma((TILES, 2)),
            dma((CHUNKS,)),
            dma((CHUNKS, partners)),
            dma((CHUNKS, PARTS)),
            dma((TILES,)),
            dma((TILES, partners)),
            dma((TILES, PARTS)),
            dma((TILES, 2)),
            dma((TILES, 2)),
            dma((4,)),
        ],
        compiler_params=pltpu.CompilerParams(
            collective_id=0, has_side_effects=True, vmem_limit_bytes=VMEM_LIMIT
        ),
        cost_estimate=pl.CostEstimate(
            flops=8 * 2 * LOCAL * ROWS * COLS * POINTS // 2, bytes_accessed=12 * 2**20, transcendentals=0
        ),
    )(fields.reshape(2 * LOCAL, ROWS, COLS), evaluate.T, project, feed, kill)
    stepped = pl.pallas_call(
        hand_over,
        out_shape=jax.ShapeDtypeStruct((2 * LOCAL, ROWS, COLS), F32),
        in_specs=[hbm] * 3,
        out_specs=hbm,
        scratch_shapes=[
            pltpu.VMEM((2 * LOCAL, ROWS, COLS), F32),
            pltpu.VMEM((LATE, ROWS + 2, 8, COLS), F32),
            pltpu.VMEM((3, LATE, CHUNKS, 8, 128), F32),
            pltpu.VMEM((ROWS + 2, 8, COLS), F32),
            pltpu.VMEM((ROWS + 2, 8, COLS), F32),
            pltpu.VMEM((2, 8 * LATE * ROWS, 128), F32),
            dma((SWEPT,)),
            dma((2,)),
            dma((SWEPT,)),
            dma((LATE, 2)),
        ],
        compiler_params=pltpu.CompilerParams(vmem_limit_bytes=VMEM_LIMIT),
    )(stepped, rs, edges)
    return stepped.reshape(2, LOCAL, ROWS, COLS)


def solution(mesh):
    in_specs = (P(None, "mode", None, "col"), P(), P(), P(), P())
    out_specs = P(None, "mode", None, "col")
    return jax.shard_map(body, mesh=mesh, in_specs=in_specs, out_specs=out_specs, check_vma=False)
```

```python
import jax
import jax.numpy as jnp
from jax import lax
from jax.experimental import pallas as pl
from jax.experimental.pallas import tpu as pltpu
from jax.sharding import PartitionSpec as P

MESH = pl.DeviceIdType.MESH
F32, BF16 = jnp.float32, jnp.bfloat16

VMEM_LIMIT = 58 * 2**20
TIME_STEP = 0.5
DIFFUSION = (1.0, 0.5)

MODES, POINTS = 288, 1584
PARTS = 8
LOCAL = 36
ROWS, COLS = 64, 256
CHUNKS = 4
TILES = 9
MESSAGE = 144
DEPTH = 384
PADDED = 1664
BLOCK = 528
OUT_ROWS = 320
WINDOW = 3
LAG = 2
LATE = 1
SWEPT = TILES - LATE
EARLY = 3
PARTNERS = ((0, 1), (1, 0), (3, 0), (2, 0), (1, 1), (3, 1), (2, 1))


def iota(shape, dim):
    return lax.broadcasted_iota(jnp.int32, shape, dim)


def sweep_tile(g, start, own_edge, left_edge, right_edge, ita, itb, fv, place):
    lane = iota((8, 128), 1)
    pair = 8 * g + iota((8, 128), 0)
    weight = jnp.where(pair < LOCAL, DIFFUSION[0], DIFFUSION[1])
    keep = 1.0 / (1.0 + 4.0 * weight)
    near = weight / (1.0 + 4.0 * weight)

    low = (lane & 7) < 4
    lefts = [jnp.where(low, left_edge[c], own_edge[c]) for c in range(CHUNKS)]
    rights = [jnp.where(low, own_edge[c], right_edge[c]) for c in range(CHUNKS)]
    left_base, right_base = lefts, rights

    def seam(now, base):
        later = []
        downs = [pltpu.roll(x, 8, 1) for x in now]
        ups = [pltpu.roll(x, 120, 1) for x in now]
        for c in range(CHUNKS):
            total = jnp.where(lane < 8, downs[c - 1] if c else 0.0, downs[c])
            total = total + jnp.where(lane >= 120, ups[c + 1] if c + 1 < CHUNKS else 0.0, ups[c])
            total = total + (pltpu.roll(now[c], 1, 1) + pltpu.roll(now[c], 127, 1))
            later.append(keep * base[c] + near * total)
        return later

    def row(ref, r):
        return [ref[r, :, :128], ref[r, :, 128:]]

    def sweep(source, store):
        beside = [
            jnp.where((lane & 7) == 3, x, pltpu.roll(y, 126, 1)) for x, y in zip(lefts, rights, strict=True)
        ]
        up, middle = row(source, 0), row(source, 1)
        for r in range(1, ROWS + 1):
            down = row(source, r + 1)
            base = row(start, r) if source is not start else middle
            after = [pltpu.roll(t, 1, 1) for t in middle]
            before = [pltpu.roll(t, 127, 1) for t in middle]
            edge = pltpu.roll(beside[(r - 1) // 16], (125 - 8 * ((r - 1) % 16)) % 128, 1)
            sides = [
                jnp.where(lane == 0, edge, after[0]) + jnp.where(lane == 127, before[1], before[0]),
                jnp.where(lane == 0, after[0], after[1]) + jnp.where(lane == 127, edge, before[1]),
            ]
            store(r, [keep * base[t] + near * ((up[t] + down[t]) + sides[t]) for t in range(2)])
            up, middle = middle, down

    def into(ref):
        def store(r, result):
            ref[r, :, :128] = result[0]
            ref[r, :, 128:] = result[1]

        return store

    def last_store(r, result):
        rows = pl.ds(8 * place * ROWS + r - 1, 8, stride=ROWS)
        fv[0, rows, :] = result[0]
        fv[1, rows, :] = result[1]

    source = start
    for store_ref in (ita, itb, ita):
        sweep(source, into(store_ref))
        source = store_ref
        lefts, rights = seam(lefts, left_base), seam(rights, right_base)
    sweep(source, last_store)


def kernel(
    fields, evaluate, project, feed, kill, out, rs_out, edge_out,
    fv, ft, ita, itb, ev, pj, weights, proj, rate_b,
    snd, rcv, reacted, bsnd, brcv, hsnd, hrcv,
    in_sem, table_sem, out_sem, own_sem, fs_sem, fr_sem, bown_sem, bs_sem, br_sem, hs_sem, hr_sem, late_sem,
):
    me, col = lax.axis_index("mode"), lax.axis_index("col")
    cols = lax.axis_size("col")
    right, left = (col + 1) % cols, (col + cols - 1) % cols
    partners = [((me // 2 + dy) % 4) * 2 + (me % 2 + dx) % 2 for dy, dx in PARTNERS]

    barrier = pltpu.get_barrier_semaphore()
    for part in partners:
        pl.semaphore_signal(barrier, inc=1, device_id=(part, col), device_id_type=MESH)
    for side in (right, left):
        pl.semaphore_signal(barrier, inc=1, device_id=(me, side), device_id_type=MESH)

    planes = fv.reshape(2, 2 * LOCAL, ROWS, 128)

    def load(chunk, half):
        rows = pl.ds(16 * chunk, 16)
        return pltpu.make_async_copy(
            fields.at[:, rows, pl.ds(128 * half, 128)], planes.at[half, :, rows, :], in_sem.at[chunk, half]
        )

    for chunk in range(CHUNKS):
        for half in range(2):
            load(chunk, half).start()
    tables = [
        pltpu.make_async_copy(evaluate, ev, table_sem.at[0]),
        pltpu.make_async_copy(project, pj, table_sem.at[1]),
    ]
    for table in tables:
        table.start()

    def prepare(chunk):
        def one(dest, carry):
            row = 16 * chunk + 2 * dest
            values = []
            for j in range(2):
                values.append([])
                for g in range(TILES):
                    rows = pl.ds(8 * g * ROWS + row + j, 8, stride=ROWS)
                    values[j].append(jnp.concatenate([fv[0, rows, :], fv[1, rows, :]], axis=1))
                for g in range(TILES):
                    ft[g, row + j + 1, :, :COLS] = values[j][g]
            for j in range(2):
                for k, g in enumerate((0, 2, 5, 7)):
                    pair = jnp.concatenate([values[j][g], values[j][g + 1]], axis=0)
                    snd[dest, chunk, 64 * j + 16 * k : 64 * j + 16 * k + 16, :] = pair.astype(BF16)
            pair = jnp.concatenate([values[0][4], values[1][4]], axis=0)
            snd[dest, chunk, 128:144, :] = pair.astype(BF16)
            return carry

        lax.fori_loop(0, PARTS, one, 0)

    def forward(chunk, k):
        part = partners[k]
        return pltpu.make_async_remote_copy(
            src_ref=snd.at[part, chunk], dst_ref=rcv.at[chunk, me],
            send_sem=fs_sem.at[chunk, k], recv_sem=fr_sem.at[chunk, me],
            device_id=(part, col), device_id_type=MESH,
        )

    def forward_in(chunk, k):
        part = partners[k]
        return pltpu.make_async_remote_copy(
            src_ref=snd.at[part, chunk], dst_ref=rcv.at[chunk, part],
            send_sem=fs_sem.at[chunk, k], recv_sem=fr_sem.at[chunk, part],
            device_id=(part, col), device_id_type=MESH,
        )

    def own(chunk):
        return pltpu.make_async_copy(snd.at[me, chunk], rcv.at[chunk, me], own_sem.at[chunk])

    for half in range(2):
        load(0, half).wait()
    prepare(0)
    pl.semaphore_wait(barrier, len(PARTNERS) + 2)
    for chunk in range(CHUNKS):
        if chunk > 0:
            for half in range(2):
                load(chunk, half).wait()
            prepare(chunk)
        for k in range(len(PARTNERS)):
            forward(chunk, k).start()
        own(chunk).start()

    for g in range(TILES):
        ft[g, 0, :, :] = jnp.zeros((8, COLS), F32)
        ft[g, ROWS + 1, :, :] = jnp.zeros((8, COLS), F32)
    for ref in (ita, itb):
        ref[0, :, :] = jnp.zeros((8, COLS), F32)
        ref[ROWS + 1, :, :] = jnp.zeros((8, COLS), F32)
    for table in tables:
        table.wait()
    mode = iota((MODES, DEPTH), 0)
    slot = iota((MODES, DEPTH), 1)
    mixed = slot - 256
    for f in range(2):
        main_mode = LOCAL * (slot >> 5) + (slot & 31) + 4 * f
        place = mixed & 7
        mix_mode = LOCAL * (mixed >> 4) + (place - 4 if f else place + 32)
        for j in range(2):
            mine = (((mixed >> 3) & 1) == j) & ((place >= 4) if f else (place < 4))
            want = jnp.where(slot < 256, main_mode, jnp.where(mine, mix_mode, -1))
            onehot = jnp.where(want == mode, 1.0, 0.0).astype(BF16)
            weights[2 * f + j] = lax.dot_general(
                ev[...], onehot, (((0,), (0,)), ((), ())), preferred_element_type=F32
            ).astype(BF16)
    mode = iota((OUT_ROWS, MODES), 1)
    slot = iota((OUT_ROWS, MODES), 0)
    mixed = slot - 256
    for f in range(2):
        main_mode = LOCAL * (slot >> 5) + (slot & 31) + 4 * f
        place = mixed & 7
        mix_mode = LOCAL * (mixed >> 3) + (place - 4 if f else place + 32)
        mine = (place >= 4) if f else (place < 4)
        want = jnp.where(slot < 256, main_mode, jnp.where(mine, mix_mode, -1))
        onehot = jnp.where(want == mode, 1.0, 0.0).astype(BF16)
        proj[f, :, 1536:] = jnp.zeros((OUT_ROWS, 128), BF16)
        proj[f, :, :POINTS] = jnp.dot(onehot, pj[...], preferred_element_type=F32).astype(BF16)
        reacted[f, POINTS:, :] = jnp.zeros((PADDED - POINTS, 2 * COLS), BF16)
    eye = iota((128, 128), 0) == iota((128, 128), 1)
    for q in (*range(0, POINTS - 128, 128), POINTS - 128):
        supply = feed[q : q + 128].reshape(1, 128)
        for f, rate in enumerate((supply, supply + kill[q : q + 128].reshape(1, 128))):
            column = jnp.sum(jnp.where(eye, jnp.broadcast_to(rate, (128, 128)), 0.0), axis=1, keepdims=True)
            rate_b[f, q : q + 128, :] = jnp.broadcast_to(column, (128, 128))

    def arrive(chunk):
        for k in range(len(PARTNERS)):
            forward_in(chunk, k).wait_recv()
        own(chunk).wait()

    def react(chunk):
        def block(b, carry):
            rows = pl.ds(pl.multiple_of(b * BLOCK, 16), BLOCK)
            feed = jnp.tile(rate_b[0, rows, :], (1, 2))
            loss = jnp.tile(rate_b[1, rows, :], (1, 2))
            for j in range(2):
                mix = rcv[chunk, :, 128:144, :].reshape(128, COLS)
                ub = jnp.concatenate([rcv[chunk, :, 64 * j : 64 * j + 32, :].reshape(256, COLS), mix], axis=0)
                vb = jnp.concatenate([rcv[chunk, :, 64 * j + 32 : 64 * j + 64, :].reshape(256, COLS), mix], axis=0)
                u = jnp.dot(weights[j, rows, :], ub, preferred_element_type=F32)
                v = jnp.dot(weights[2 + j, rows, :], vb, preferred_element_type=F32)
                squared = u * v * v
                lanes = slice(COLS * j, COLS * j + COLS)
                reacted[0, rows, lanes] = (feed * (1.0 - u) - squared).astype(BF16)
                reacted[1, rows, lanes] = (squared - loss * v).astype(BF16)
            return carry

        lax.fori_loop(0, POINTS // BLOCK, block, 0)

    def project_back(chunk):
        mix = None
        for f in range(2):
            total = jnp.dot(proj[f], reacted[f], preferred_element_type=F32)
            main = jnp.stack(
                [total[:256, :COLS].reshape(32, 8, COLS), total[:256, COLS:].reshape(32, 8, COLS)], axis=1
            ).astype(BF16)
            bsnd[:, 5 * f : 5 * f + 4, chunk] = main.reshape(PARTS, 4, 16, COLS)
            mix = total[256:] if f == 0 else mix + total[256:]
        mix = jnp.stack([mix[:, :COLS].reshape(8, 8, COLS), mix[:, COLS:].reshape(8, 8, COLS)], axis=1)
        bsnd[:, 4, chunk] = mix.astype(BF16).reshape(PARTS, 16, COLS)

    def backward(g, k, low=0, high=CHUNKS, incoming=False):
        part = partners[k]
        slot = part if incoming else me
        return pltpu.make_async_remote_copy(
            src_ref=bsnd.at[part, g, low:high], dst_ref=brcv.at[slot, g, low:high],
            send_sem=bs_sem.at[g, k], recv_sem=br_sem.at[g, slot],
            device_id=(part, col), device_id_type=MESH,
        )

    def back_own(g, low=0, high=CHUNKS):
        return pltpu.make_async_copy(bsnd.at[me, g, low:high], brcv.at[me, g, low:high], bown_sem.at[g])

    def send_back(g, low=0, high=CHUNKS):
        for k in range(len(PARTNERS)):
            backward(g, k, low, high).start()
        back_own(g, low, high).start()

    def work(chunk):
        react(chunk)
        project_back(chunk)

    def early(chunk, carry):
        arrive(chunk)
        work(chunk)
        return carry

    lax.fori_loop(0, CHUNKS - 1, early, 0)
    arrive(CHUNKS - 1)
    for g in range(EARLY):
        send_back(g, 0, CHUNKS - 1)
    work(CHUNKS - 1)
    for g in range(EARLY):
        send_back(g, CHUNKS - 1, CHUNKS)
    for g in range(EARLY, WINDOW):
        send_back(g)

    lane = iota((8, 128), 1)

    def gather(g):
        for k in range(len(PARTNERS)):
            backward(g, k, incoming=True).wait_recv()
        back_own(g).wait()

        def rows16(c, carry):
            packed = jnp.zeros((8, 128), F32)
            for s in range(PARTS):
                pair = brcv[s, g, c].astype(F32)
                for j in range(2):
                    row = 16 * c + 2 * s + j + 1
                    value = ft[g, row, :, :COLS] + TIME_STEP * pair[8 * j : 8 * j + 8]
                    ft[g, row, :, :COLS] = value
                    edge = jnp.where(lane < 64, value[:, :128], value[:, 128:])
                    at = 2 * s + j
                    packed = jnp.where((lane >> 3) == at, pltpu.roll(edge, (8 * at + 4) % 128, 1), packed)
            hsnd[g, c] = packed
            return carry

        lax.fori_loop(0, CHUNKS, rows16, 0)

    def halo(g, side, incoming=False):
        there = 1 - side if incoming else side
        return pltpu.make_async_remote_copy(
            src_ref=hsnd.at[g], dst_ref=hrcv.at[there, g],
            send_sem=hs_sem.at[g, side], recv_sem=hr_sem.at[g, there],
            device_id=(me, left if side else right), device_id_type=MESH,
        )

    def sweeps(g):
        for side in range(2):
            halo(g, side, True).wait_recv()
        own_edge, left_edge, right_edge = [
            [part[c] for c in range(CHUNKS)] for part in (hsnd.at[g], hrcv.at[0, g], hrcv.at[1, g])
        ]
        sweep_tile(g, ft.at[g], own_edge, left_edge, right_edge, ita, itb, fv, g)

    def write(g, half):
        rows = pl.ds(8 * g, 8)
        return pltpu.make_async_copy(
            planes.at[half, rows], out.at[rows, :, pl.ds(128 * half, 128)], out_sem.at[g, half]
        )

    def turn(i, carry):
        @pl.when(i < TILES)
        def _():
            gather(i)
            for side in range(2):
                halo(i, side).start()

        @pl.when(i + WINDOW < TILES)
        def _():
            send_back(i + WINDOW)

        @pl.when(i >= LAG)
        def _():
            sweeps(i - LAG)
            for half in range(2):
                write(i - LAG, half).start()

        return carry

    lax.fori_loop(0, TILES + LAG - LATE, turn, 0)

    late = [pltpu.make_async_copy(ft.at[SWEPT:], rs_out, late_sem.at[0])]
    late.append(pltpu.make_async_copy(hsnd.at[SWEPT:], edge_out.at[0], late_sem.at[1]))
    for side in range(2):
        late.append(pltpu.make_async_copy(hrcv.at[side, SWEPT:], edge_out.at[1 + side], late_sem.at[2 + side]))
    for copy in late[:2]:
        copy.start()
    for g in range(SWEPT, TILES):
        for side in range(2):
            halo(g, side, True).wait_recv()
    for copy in late[2:]:
        copy.start()

    for chunk in range(CHUNKS):
        for k in range(len(PARTNERS)):
            forward(chunk, k).wait_send()

    def finish(g, carry):
        for k in range(len(PARTNERS)):
            backward(g, k).wait_send()
        for side in range(2):
            halo(g, side).wait_send()

        @pl.when(g < SWEPT)
        def _():
            for half in range(2):
                write(g, half).wait()

        return carry

    lax.fori_loop(0, TILES, finish, 0)
    for copy in late:
        copy.wait()


def hand_over(source, rs, edges, target, held, ft, near, ita, itb, fv, in_sem, late_sem, out_sem, done_sem):
    first = [pltpu.make_async_copy(rs, ft, late_sem.at[0]), pltpu.make_async_copy(edges, near, late_sem.at[1])]
    rows = [pl.ds(8 * g, 8) for g in range(TILES)]
    reads = [pltpu.make_async_copy(source.at[rows[g]], held.at[rows[g]], in_sem.at[g]) for g in range(SWEPT)]
    writes = [pltpu.make_async_copy(held.at[rows[g]], target.at[rows[g]], out_sem.at[g]) for g in range(SWEPT)]
    for copy in first + reads:
        copy.start()
    for ref in (ita, itb):
        ref[0, :, :] = jnp.zeros((8, COLS), F32)
        ref[ROWS + 1, :, :] = jnp.zeros((8, COLS), F32)
    for copy in first:
        copy.wait()
    for read, write in zip(reads, writes, strict=True):
        read.wait()
        write.start()
    planes = fv.reshape(2, 8 * LATE, ROWS, 128)
    last = []
    for i in range(LATE):
        own_edge, left_edge, right_edge = [[near[k, i, c] for c in range(CHUNKS)] for k in range(3)]
        sweep_tile(SWEPT + i, ft.at[i], own_edge, left_edge, right_edge, ita, itb, fv, i)
        for half in range(2):
            lanes = pl.ds(128 * half, 128)
            copy = pltpu.make_async_copy(
                planes.at[half, pl.ds(8 * i, 8)], target.at[rows[SWEPT + i], :, lanes], done_sem.at[i, half]
            )
            copy.start()
            last.append(copy)
    for copy in writes + last:
        copy.wait()


def body(fields, evaluate, project, feed, kill):
    partners = len(PARTNERS)
    hbm = pl.BlockSpec(memory_space=pltpu.MemorySpace.HBM)
    vmem = pl.BlockSpec(memory_space=pltpu.VMEM)
    dma = pltpu.SemaphoreType.DMA
    stepped, rs, edges = pl.pallas_call(
        kernel,
        out_shape=[
            jax.ShapeDtypeStruct((2 * LOCAL, ROWS, COLS), F32),
            jax.ShapeDtypeStruct((LATE, ROWS + 2, 8, COLS), F32),
            jax.ShapeDtypeStruct((3, LATE, CHUNKS, 8, 128), F32),
        ],
        in_specs=[hbm, hbm, hbm, vmem, vmem],
        out_specs=[hbm] * 3,
        scratch_shapes=[
            pltpu.VMEM((2, 2 * LOCAL * ROWS, 128), F32),
            pltpu.VMEM((TILES, ROWS + 2, 8, COLS), F32),
            pltpu.VMEM((ROWS + 2, 8, COLS), F32),
            pltpu.VMEM((ROWS + 2, 8, COLS), F32),
            pltpu.VMEM((MODES, POINTS), BF16),
            pltpu.VMEM((MODES, POINTS), BF16),
            pltpu.VMEM((4, POINTS, DEPTH), BF16),
            pltpu.VMEM((2, OUT_ROWS, PADDED), BF16),
            pltpu.VMEM((2, POINTS, 128), F32),
            pltpu.VMEM((PARTS, CHUNKS, MESSAGE, COLS), BF16),
            pltpu.VMEM((CHUNKS, PARTS, MESSAGE, COLS), BF16),
            pltpu.VMEM((2, PADDED, 2 * COLS), BF16),
            pltpu.VMEM((PARTS, TILES, CHUNKS, 16, COLS), BF16),
            pltpu.VMEM((PARTS, TILES, CHUNKS, 16, COLS), BF16),
            pltpu.VMEM((TILES, CHUNKS, 8, 128), F32),
            pltpu.VMEM((2, TILES, CHUNKS, 8, 128), F32),
            dma((CHUNKS, 2)),
            dma((2,)),
            dma((TILES, 2)),
            dma((CHUNKS,)),
            dma((CHUNKS, partners)),
            dma((CHUNKS, PARTS)),
            dma((TILES,)),
            dma((TILES, partners)),
            dma((TILES, PARTS)),
            dma((TILES, 2)),
            dma((TILES, 2)),
            dma((4,)),
        ],
        compiler_params=pltpu.CompilerParams(
            collective_id=0, has_side_effects=True, vmem_limit_bytes=VMEM_LIMIT
        ),
        cost_estimate=pl.CostEstimate(
            flops=8 * 2 * LOCAL * ROWS * COLS * POINTS // 2, bytes_accessed=12 * 2**20, transcendentals=0
        ),
    )(fields.reshape(2 * LOCAL, ROWS, COLS), evaluate.T, project, feed, kill)
    stepped = pl.pallas_call(
        hand_over,
        out_shape=jax.ShapeDtypeStruct((2 * LOCAL, ROWS, COLS), F32),
        in_specs=[hbm] * 3,
        out_specs=hbm,
        scratch_shapes=[
            pltpu.VMEM((2 * LOCAL, ROWS, COLS), F32),
            pltpu.VMEM((LATE, ROWS + 2, 8, COLS), F32),
            pltpu.VMEM((3, LATE, CHUNKS, 8, 128), F32),
            pltpu.VMEM((ROWS + 2, 8, COLS), F32),
            pltpu.VMEM((ROWS + 2, 8, COLS), F32),
            pltpu.VMEM((2, 8 * LATE * ROWS, 128), F32),
            dma((SWEPT,)),
            dma((2,)),
            dma((SWEPT,)),
            dma((LATE, 2)),
        ],
        compiler_params=pltpu.CompilerParams(vmem_limit_bytes=VMEM_LIMIT),
    )(stepped, rs, edges)
    return stepped.reshape(2, LOCAL, ROWS, COLS)


def solution(mesh):
    in_specs = (P(None, "mode", None, "col"), P(), P(), P(), P())
    out_specs = P(None, "mode", None, "col")
    return jax.shard_map(body, mesh=mesh, in_specs=in_specs, out_specs=out_specs, check_vma=False)
```
